256 devices in a mesh: dp: 32 (over x, y, core), seq: 8 (over z).
Axes of the slice: x: 4, y: 4, z: 8, core: 2. Of those that a mesh axis runs over, the one named last changes fastest.
Arguments:
- queries: bfloat16 [32768, 8192], P(('dp', 'seq')), may hold values from -600 to 600
- output_gradient: bfloat16 [32768, 8192], P(('dp', 'seq')), may hold values from -6 to 6
- tiles: bfloat16 [512, 32, 7680], P('dp', None, 'seq'), may hold values from -6 to 6
- frozen_key_weight: bfloat16 [7680, 1024], P('seq'), may hold values from -0.0625 to 0.0625
- frozen_value_weight: bfloat16 [7680, 1024], P('seq'), may hold values from -0.0625 to 0.0625
- key_norm_gain: float32 [128], replicated, may hold values from 0.1 to 1.9
- adapter_down_weight: bfloat16 [7680, 16], P('seq'), may hold values from -0.0625 to 0.0625
- adapter_up_weight: bfloat16 [16, 1024], P(None, 'seq'), may hold values from -1.5 to 1.5
- gate: float32 [1], replicated, may hold values from 0.3 to 1.5
- document_lengths: int32 [32, 4], P('dp'), may hold values from 1 to 512, 1024 in all within a row
- image_reader_group: int32 [512], P('dp'), may hold values from 0 to 31, as said below
- image_document: int32 [512], P('dp'), may hold values from 0 to 3, as said below
Outputs:
- gated: bfloat16 [32768, 8192], P(('dp', 'seq'))
- query_grad: bfloat16 [32768, 8192], P(('dp', 'seq'))
- down_grad: float32 [7680, 16], P('seq')
- up_weight_gradient: float32 [16, 1024], P(None, 'seq')
The draws below stay inside these ranges and needn't reach their ends.
Inputs may be any that keep to these rules, and one draw needn't show every extreme that they name: `image_reader_group`: the 16 images of one encoder shard go to 16 different groups; every group reads at least 4 images. `image_document`: every document of every group has at least one image.
All inputs are finite; a program needn't handle non-finite values.
Results may differ from the reference program's by a relative error of at most 0.029.
The reference program's roundings to bfloat16 on the way count: a program that leaves them out, or rounds other values in their place, can miss the bound.
Values may be sent and summed in bfloat16 or wider, within the bound.
A program may use at most 192 MiB of HBM per device.

```python
import math
import jax
import jax.numpy as jnp
import numpy as np
from jax import lax

HQ = 64
KEY_VALUE_HEADS = 8
HEAD_SIZE = 128
VISION_WIDTH = 7680
ADAPTER_RANK = 16
DOCS = 4
TOK_DEV = 128
IMG_DEV = 16
IMG_ROWS = 32
IMAGES = 512
SEQ_TOK = 1024
TOKENS = 32768
N_DP = 32
N_SEQ = 8


def route_tables(key):
    offset_key, score_key = jax.random.split(key)
    shifts = jax.random.permutation(offset_key, N_DP)[:DOCS].astype(jnp.int32)
    owners = jnp.arange(N_DP, dtype=jnp.int32)
    required = jnp.any((owners[:, None, None] + shifts[None, None, :]) % N_DP == owners[None, :, None], axis=2)
    random_part = jax.random.randint(score_key, (N_DP, N_DP), 0, 65536).astype(jnp.int32)
    scores = random_part * N_DP + owners[None, :] + required.astype(jnp.int32) * (1 << 24)
    unused, chosen = lax.top_k(scores, IMG_DEV)
    chosen = chosen.astype(jnp.int32)
    onehot = (chosen[:, :, None] == owners[None, None, :]).astype(jnp.int32)
    sent_counts = jnp.sum(onehot, axis=1)
    before = jnp.cumsum(sent_counts, axis=0) - sent_counts
    arrival = jnp.sum(onehot * before[:, None, :], axis=2)
    doc_index = arrival % DOCS
    return (chosen.reshape(-1), doc_index.reshape(-1).astype(jnp.int32))


def draw_image_reader_group(key, part):
    chosen, doc_index = route_tables(key)
    return chosen


def draw_image_document(key, part):
    chosen, doc_index = route_tables(key)
    return doc_index


def draw_queries(key, part):
    key = jax.random.fold_in(key, 5)
    base_key = jax.random.fold_in(key, 0)
    base = jax.random.normal(base_key, (TOKENS, HQ * HEAD_SIZE), jnp.float32)
    values = jnp.clip(base, -6.0, 6.0)
    return values.astype(jnp.bfloat16)


def shard_levels(stream_key, dims, cuts, low, top_value):
    def one(dim, blocks):
        heights = jax.random.uniform(jax.random.fold_in(jax.random.fold_in(stream_key, 6), dim), (blocks,), jnp.float32, low / len(cuts), top_value / len(cuts))
        return jnp.repeat(jnp.exp(heights), dims[dim] // blocks).reshape((-1,) + (1,) * (len(dims) - dim - 1))

    level = one(*cuts[0])
    for cut in cuts[1:]:
        level = level * one(*cut)
    return level


def split_up(number_of, total, most, skew):
    weights = [(1 << 20) // math.isqrt(rank ** skew) + 1 for rank in range(2, number_of + 1)]
    rest, holding = total - most - (number_of - 1), [1] * (number_of - 1)
    while rest > 0:
        free = [i for i in range(number_of - 1) if holding[i] < most]
        whole, left = sum([weights[i] for i in free]), rest
        for i in free:
            extra = min(most - holding[i], max(1, left * weights[i] // whole), rest)
            holding[i] = holding[i] + extra
            rest = rest - extra
    return np.array([most] + holding)


def uneven_parts(stream_key, amount, total, most, lean):
    if amount == 2:
        one = jax.random.randint(stream_key, (), max(1, total - most), min(most, total - 1) + 1)
        return jnp.stack([one, total - one])
    sizes = jnp.asarray(split_up(amount, total, most, lean), jnp.int32)
    pairs = (amount - 1) // 2
    giver, receiver = sizes[1:1 + 2 * pairs:2], sizes[2:2 + 2 * pairs:2]
    room = jnp.minimum(giver - 1, most - receiver)
    moved = jax.random.randint(jax.random.fold_in(stream_key, 1), (pairs,), 0, 1 << 20) % (room + 1)
    sizes = sizes.at[1:1 + 2 * pairs:2].set(giver - moved).at[2:2 + 2 * pairs:2].set(receiver + moved)
    return sizes[jax.random.permutation(jax.random.fold_in(stream_key, 2), amount)]


def bell_draw(stream_key, shape, width, most, cuts=(), kind=jnp.bfloat16):
    values = jax.random.normal(stream_key, shape, jnp.float32) * width
    if len(cuts) > 0:
        values = shard_levels(stream_key, shape, cuts, -0.22, 0.18) * values
    return jnp.clip(values, min=-most, max=most).astype(kind)


def setup_inputs(seed: int = 0) -> dict:
    key_list = jax.random.split(jax.random.key(seed), 13)
    queries = draw_queries(jax.random.fold_in(key_list[12], 71), 0)
    output_gradient = bell_draw(key_list[1], (TOKENS, HQ * HEAD_SIZE), 1.0, 6.0, ((0, 256),))
    tiles = bell_draw(key_list[2], (IMAGES, IMG_ROWS, VISION_WIDTH), 1.0, 6.0, ((0, 32), (2, 8)))
    frozen_key_weight = bell_draw(key_list[3], (VISION_WIDTH, KEY_VALUE_HEADS * HEAD_SIZE), VISION_WIDTH ** -0.5, 0.0625, ((0, 8),))
    frozen_value_weight = bell_draw(key_list[4], (VISION_WIDTH, KEY_VALUE_HEADS * HEAD_SIZE), VISION_WIDTH ** -0.5, 0.0625, ((0, 8),))
    key_norm_gain = jnp.clip(1.0 + 0.18 * jax.random.normal(key_list[5], (HEAD_SIZE,), jnp.float32), 0.1, 1.9)
    adapter_down_weight = bell_draw(key_list[6], (VISION_WIDTH, ADAPTER_RANK), VISION_WIDTH ** -0.5, 0.0625, ((0, 8),))
    adapter_up_weight = bell_draw(key_list[7], (ADAPTER_RANK, KEY_VALUE_HEADS * HEAD_SIZE), ADAPTER_RANK ** -0.5, 1.5, ((1, 8),))
    gate = jnp.clip(jax.random.uniform(key_list[8], (1,), jnp.float32, 0.3, 1.5), 0.3, 1.5)
    document_lengths = jax.vmap(lambda own: uneven_parts(own, DOCS, TOK_DEV * N_SEQ, TOK_DEV * N_SEQ // 2, 2))(jax.random.split(key_list[9], N_DP)).reshape((N_DP, DOCS)).astype(jnp.int32)
    image_reader_group = draw_image_reader_group(jax.random.fold_in(key_list[12], 71), 0)
    image_document = draw_image_document(jax.random.fold_in(key_list[12], 71), 0)
    return dict(queries=queries, output_gradient=output_gradient, tiles=tiles, frozen_key_weight=frozen_key_weight, frozen_value_weight=frozen_value_weight, key_norm_gain=key_norm_gain, adapter_down_weight=adapter_down_weight, adapter_up_weight=adapter_up_weight, gate=gate, document_lengths=document_lengths, image_reader_group=image_reader_group, image_document=image_document)


EPS = 1e-05
ADAPTER_SCALE = 2.0

def attend(queries, attn_grad, key_rows, value_matrix_rows, tok_doc, key_doc, gate_value):
    num_rows = queries.shape[0]
    kv_heads, key_count, head_extent = key_rows.shape
    group_size = queries.shape[1] // (kv_heads * head_extent)
    score_scale = head_extent ** (-0.5)
    block_rows = min(512, num_rows)
    query_four = queries.reshape(num_rows, kv_heads, group_size, head_extent)
    grad_four = attn_grad.reshape(num_rows, kv_heads, group_size, head_extent)
    gated_parts = []
    qgrad_parts = []
    value_sums = [jnp.zeros((key_count, head_extent), jnp.float32) for head in range(kv_heads)]
    for first_row in range(0, num_rows, block_rows):
        allowed = tok_doc[first_row:first_row + block_rows, None] == key_doc[None, :]
        gated_heads = []
        qgrad_heads = []
        for head in range(kv_heads):
            query_block = query_four[first_row:first_row + block_rows, head].astype(jnp.float32)
            grad_block = grad_four[first_row:first_row + block_rows, head].astype(jnp.float32)
            keys_f = key_rows[head].astype(jnp.float32)
            values_f = value_matrix_rows[head].astype(jnp.float32)
            scores = jnp.einsum('ngd,md->gnm', query_block, keys_f) * score_scale
            scores = jnp.where(allowed[None], scores, -1e+30)
            row_max = lax.optimization_barrier(jnp.max(scores, axis=-1, keepdims=True))
            weights = jnp.exp(scores - row_max)
            prob_f32 = weights / lax.optimization_barrier(jnp.sum(weights, axis=-1, keepdims=True))
            prob_bf16 = prob_f32.astype(jnp.bfloat16)
            prob_used = prob_bf16.astype(jnp.float32)
            attended = jnp.einsum('gnm,md->ngd', prob_used, values_f)
            gated_heads.append((gate_value * attended).astype(jnp.bfloat16))
            row_delta = lax.optimization_barrier(jnp.sum(grad_block * attended, axis=-1))
            prob_grad = jnp.einsum('ngd,md->gnm', grad_block, values_f)
            score_grad = (prob_f32 * (prob_grad - row_delta.T[:, :, None])).astype(jnp.bfloat16)
            query_grad = jnp.einsum('gnm,md->ngd', score_grad.astype(jnp.float32), keys_f) * score_scale
            qgrad_heads.append(query_grad.astype(jnp.bfloat16))
            value_sums[head] = value_sums[head] + jnp.einsum('gnm,ngd->md', prob_used, grad_block)
        gated_parts.append(jnp.stack(gated_heads, axis=1))
        qgrad_parts.append(jnp.stack(qgrad_heads, axis=1))
    gated = jnp.concatenate(gated_parts, axis=0).reshape(num_rows, -1)
    query_grad = jnp.concatenate(qgrad_parts, axis=0).reshape(num_rows, -1)
    return (gated, query_grad, jnp.stack(value_sums, axis=0))

def reference(queries, output_gradient, tiles, frozen_key_weight, frozen_value_weight, key_norm_gain, adapter_down_weight, adapter_up_weight, gate, document_lengths, image_reader_group, image_document):
    flattened_rows = tiles.reshape(IMAGES * IMG_ROWS, VISION_WIDTH)
    key_raw = jnp.dot(flattened_rows, frozen_key_weight, preferred_element_type=jnp.float32).reshape(-1, KEY_VALUE_HEADS, HEAD_SIZE)
    mean_square = lax.optimization_barrier(jnp.mean(key_raw * key_raw, axis=-1, keepdims=True))
    key_rows = (key_raw * lax.rsqrt(mean_square + EPS) * key_norm_gain).astype(jnp.bfloat16)
    reduced_rows = jnp.dot(flattened_rows, adapter_down_weight, preferred_element_type=jnp.float32).astype(jnp.bfloat16)
    value_complete = jnp.dot(flattened_rows, frozen_value_weight, preferred_element_type=jnp.float32)
    value_complete = value_complete + ADAPTER_SCALE * jnp.dot(reduced_rows, adapter_up_weight, preferred_element_type=jnp.float32)
    value_matrix_rows = value_complete.astype(jnp.bfloat16).reshape(-1, KEY_VALUE_HEADS, HEAD_SIZE)
    key_value = jnp.concatenate([key_rows, value_matrix_rows], axis=-1).reshape(N_DP, IMG_DEV, IMG_ROWS, KEY_VALUE_HEADS, 2 * HEAD_SIZE)
    key_value = key_value.astype(jnp.float32)
    reader_table = image_reader_group.reshape(N_DP, IMG_DEV)
    doc_table = image_document.reshape(N_DP, IMG_DEV)
    gate_value = jnp.tanh(gate[0])
    attn_grad = (gate_value * output_gradient.astype(jnp.float32)).astype(jnp.bfloat16)
    query_groups = queries.reshape(N_DP, SEQ_TOK, HQ * HEAD_SIZE)
    grad_groups = attn_grad.reshape(N_DP, SEQ_TOK, HQ * HEAD_SIZE)

    def per_group(items):
        group, query_rows, grad_rows, lengths = items
        picked = (reader_table == group).astype(jnp.float32)
        group_kv = jnp.einsum('ot,otrhc->horc', picked, key_value).astype(jnp.bfloat16)
        group_kv = group_kv.reshape(KEY_VALUE_HEADS, N_DP * IMG_ROWS, 2 * HEAD_SIZE)
        doc_tags = lax.optimization_barrier(jnp.sum(picked * (doc_table + 1).astype(jnp.float32), axis=1))
        key_doc = jnp.repeat(doc_tags, IMG_ROWS).astype(jnp.int32)
        positions = jnp.arange(SEQ_TOK, dtype=jnp.int32)
        doc_ends = jnp.cumsum(lengths)
        tok_doc = 1 + lax.optimization_barrier(jnp.sum((positions[:, None] >= doc_ends[None, :-1]).astype(jnp.int32), axis=1))
        gated_g, qgrad_g, value_g = attend(query_rows, grad_rows, group_kv[..., :HEAD_SIZE], group_kv[..., HEAD_SIZE:], tok_doc, key_doc, gate_value)
        return (gated_g, qgrad_g, value_g.reshape(KEY_VALUE_HEADS, N_DP, IMG_ROWS, HEAD_SIZE).astype(jnp.bfloat16))
    groups = jnp.arange(N_DP, dtype=jnp.int32)
    gated, query_grad, value_groups = lax.map(per_group, (groups, query_groups, grad_groups, document_lengths))
    owners = jnp.arange(N_DP, dtype=jnp.int32)
    value_images = value_groups[reader_table, :, owners[:, None]]
    value_gradient = value_images.transpose(0, 1, 3, 2, 4).reshape(IMAGES * IMG_ROWS, KEY_VALUE_HEADS * HEAD_SIZE)
    up_weight_gradient = ADAPTER_SCALE * jnp.dot(reduced_rows.T, value_gradient, preferred_element_type=jnp.float32)
    reduced_gradient = (ADAPTER_SCALE * jnp.dot(value_gradient, adapter_up_weight.T, preferred_element_type=jnp.float32)).astype(jnp.bfloat16)
    down_grad = jnp.dot(flattened_rows.T, reduced_gradient, preferred_element_type=jnp.float32)
    return (gated.reshape(TOKENS, HQ * HEAD_SIZE), query_grad.reshape(TOKENS, HQ * HEAD_SIZE), down_grad, up_weight_gradient)
```

```python
import functools

import jax
import jax.numpy as jnp
from jax import lax
from jax.experimental import pallas as pl
from jax.experimental.pallas import tpu as pltpu
from jax.sharding import PartitionSpec as P

EPS = 1e-05
ADAPTER_SCALE = 2.0
MASKED = -1e30
LANES = 128
LOG2_E = 1.4426950408889634
MESH = pl.DeviceIdType.MESH
NT = (((1,), (1,)), ((), ()))
TN = (((0,), (0,)), ((), ()))


def remote(src, dst, send_sem, recv_sem, target):
    return pltpu.make_async_remote_copy(
        src_ref=src,
        dst_ref=dst,
        send_sem=send_sem,
        recv_sem=recv_sem,
        device_id=target,
        device_id_type=MESH,
    )


def loop(first, last, body):
    def step(i, carry):
        body(i)
        return carry

    lax.fori_loop(first, last, step, 0)


def greet(barrier, target):
    pl.semaphore_signal(barrier, inc=1, device_id=target, device_id_type=MESH)


def project_kernel(
    n_dp,
    n_seq,
    docs,
    tiles_ref,
    wk_ref,
    wv_ref,
    wd_ref,
    up_ref,
    gain_ref,
    reader_ref,
    doc_ref,
    kv_ref,
    ext_ref,
    up_all_ref,
    own_k,
    own_v,
    sum_k,
    sum_v,
    low_own,
    low_send,
    low_recv,
    up_recv,
    pick,
    tag,
    rows_buf,
    out_buf,
    in_buf,
    k_ss,
    k_rs,
    v_ss,
    v_rs,
    low_ss,
    low_rs,
    up_ss,
    up_rs,
    out_ss,
    in_rs,
):
    p = lax.axis_index("dp")
    z = lax.axis_index("seq")
    rows = tiles_ref.shape[0]
    rank = up_ref.shape[0]
    img_dev = reader_ref.shape[0]
    img_rows = rows // img_dev
    half, quarter = rows // 2, rows // 4
    right = (p, lax.rem(z + 1, n_seq))
    left = (p, lax.rem(z + n_seq - 1, n_seq))

    def own_part(t):
        ahead = lax.rem(z + 2 * n_seq - 1 - t, n_seq)
        back = lax.rem(z + 1 + t, n_seq)
        for side, head in ((0, ahead), (1, back)):
            cols = pl.ds(pl.multiple_of(head * LANES, LANES), LANES)
            part = pl.ds(side * half, half)
            x = tiles_ref[part, :]
            own_k[part, :] = jnp.dot(x, wk_ref[:, cols], preferred_element_type=jnp.float32)
            own_v[part, :] = jnp.dot(x, wv_ref[:, cols], preferred_element_type=jnp.float32)

    def hop(t, s):
        target = right if s < 2 else left
        part = pl.ds(s * quarter, quarter)
        return (
            remote(sum_k.at[t, part], sum_k.at[t + 1, part], k_ss.at[t, s], k_rs.at[t, s], target),
            remote(sum_v.at[t, part], sum_v.at[t + 1, part], v_ss.at[t, s], v_rs.at[t, s], target),
        )

    def low_copy(k):
        target = (p, lax.rem(z + k, n_seq))
        return remote(low_send, low_recv.at[k], low_ss.at[k], low_rs.at[k], target)

    def up_copy(k, slot):
        target = (p, lax.rem(z + k, n_seq))
        return remote(up_ref, up_recv.at[slot], up_ss.at[k], up_rs.at[k], target)

    barrier = pltpu.get_barrier_semaphore()
    loop(1, n_seq, lambda k: greet(barrier, (p, lax.rem(z + k, n_seq))))
    loop(1, n_dp, lambda k: greet(barrier, (lax.rem(p + k, n_dp), z)))
    own_part(0)
    sum_k[0] = own_k[...]
    sum_v[0] = own_v[...].astype(jnp.bfloat16)
    pl.semaphore_wait(barrier, n_seq - 1 + n_dp - 1)
    for s in (0, 2, 1, 3):
        for copy in hop(0, s):
            copy.start()

    low_part = jnp.dot(tiles_ref[...], wd_ref[...], preferred_element_type=jnp.float32)
    low_own[...] = low_part.T
    low_send[...] = low_own[...].astype(jnp.bfloat16)
    loop(1, n_seq, lambda k: low_copy(k).start())
    loop(1, n_seq, lambda k: up_copy(k, z).start())
    up_recv[z] = up_ref[...]

    def find(g):
        at, mark = jnp.int32(0), jnp.int32(docs)
        for i in range(img_dev):
            hit = reader_ref[i] == g
            at = jnp.where(hit, i, at)
            mark = jnp.where(hit, doc_ref[i], mark)
        pick[g] = at
        tag[g] = mark

    loop(0, n_dp, find)

    def ring_step(t):
        own_part(t)
        for s in (0, 2, 1, 3):
            part = pl.ds(s * quarter, quarter)
            for copy in hop(t - 1, s):
                copy.wait_recv()
            sum_k[t, part, :] = sum_k[t, part, :] + own_k[part, :]
            total_v = sum_v[t, part, :].astype(jnp.float32) + own_v[part, :]
            sum_v[t, part, :] = total_v.astype(jnp.bfloat16)
            for copy in hop(t, s):
                copy.start()

    loop(1, n_seq - 1, ring_step)
    own_part(n_seq - 1)

    low_total = low_own[...]
    for k in range(1, n_seq):
        low_copy(k).wait_recv()
        low_total = low_total + low_recv[k].astype(jnp.float32)
    low_rank = low_total.astype(jnp.bfloat16)
    eye = lax.broadcasted_iota(jnp.int32, (rank, LANES), 0) == lax.broadcasted_iota(
        jnp.int32, (rank, LANES), 1
    )
    eye = jnp.where(eye, 1.0, 0.0).astype(jnp.bfloat16)
    low_up = lax.dot_general(low_rank, up_ref[...], TN, preferred_element_type=jnp.float32)
    low_rows = lax.dot_general(low_rank, eye, TN, preferred_element_type=jnp.float32)
    rows_buf[:, :, 2 * LANES :] = low_rows.astype(jnp.bfloat16).reshape(img_dev, img_rows, LANES)
    own_v[...] = own_v[...] + ADAPTER_SCALE * low_up

    for s in (0, 2, 1, 3):
        part = pl.ds(s * quarter, quarter)
        for copy in hop(n_seq - 2, s):
            copy.wait_recv()
        key_raw = sum_k[n_seq - 1, part, :] + own_k[part, :]
        mean_square = jnp.mean(key_raw * key_raw, axis=-1, keepdims=True)
        key_rows = key_raw * lax.rsqrt(mean_square + EPS) * gain_ref[...]
        images = pl.ds(s * (img_dev // 4), img_dev // 4)
        shape = (img_dev // 4, img_rows, LANES)
        rows_buf[images, :, :LANES] = key_rows.astype(jnp.bfloat16).reshape(shape)
        value = sum_v[n_seq - 1, part, :].astype(jnp.float32) + own_v[part, :]
        rows_buf[images, :, LANES : 2 * LANES] = value.astype(jnp.bfloat16).reshape(shape)

    def image_copy(k, slot):
        g = lax.rem(p + k, n_dp)
        return remote(out_buf.at[g], in_buf.at[slot], out_ss.at[k], in_rs.at[k], (g, z))

    lane = lax.broadcasted_iota(jnp.int32, (img_rows, LANES), 1)

    def image_block(g):
        block = rows_buf[pick[g]]
        mark = jnp.where(lane == rank + tag[g], 1.0, 0.0)
        extra = jnp.where(lane < rank, block[:, 2 * LANES :].astype(jnp.float32), mark)
        return block[:, : 2 * LANES], extra.astype(jnp.bfloat16)

    def send_image(k):
        g = lax.rem(p + k, n_dp)
        kv, extra = image_block(g)
        out_buf[g, :, : 2 * LANES] = kv
        out_buf[g, :, 2 * LANES :] = extra
        image_copy(k, p).start()

    loop(1, n_dp, send_image)
    kv, extra = image_block(p)
    own_rows = pl.ds(pl.multiple_of(p * img_rows, img_rows), img_rows)
    kv_ref[own_rows, :] = kv
    ext_ref[own_rows, :] = extra

    def take_image(k):
        source = lax.rem(p + n_dp - k, n_dp)
        image_copy(k, source).wait_recv()
        into = pl.ds(pl.multiple_of(source * img_rows, img_rows), img_rows)
        kv_ref[into, :] = in_buf[source, :, : 2 * LANES]
        ext_ref[into, :] = in_buf[source, :, 2 * LANES :]

    def take_up(k):
        up_copy(k, lax.rem(z + n_seq - k, n_seq)).wait_recv()

    loop(1, n_seq, take_up)
    up_all_ref[...] = up_recv[...]
    loop(1, n_dp, take_image)

    def sent(t):
        for s in range(4):
            for copy in hop(t, s):
                copy.wait_send()

    loop(0, n_seq - 1, sent)
    loop(1, n_seq, lambda k: low_copy(k).wait_send())
    loop(1, n_seq, lambda k: up_copy(k, z).wait_send())
    loop(1, n_dp, lambda k: image_copy(k, p).wait_send())


def project(n_dp, n_seq, docs, tiles, wk, wv, wd, up, gain, reader, doc):
    rows = tiles.shape[0]
    img_rows = rows // reader.shape[0]
    rank = up.shape[0]
    keys = n_dp * img_rows
    vmem = pl.BlockSpec(memory_space=pltpu.VMEM)
    smem = pl.BlockSpec(memory_space=pltpu.SMEM)
    f32, bf16, dma = jnp.float32, jnp.bfloat16, pltpu.SemaphoreType.DMA
    return pl.pallas_call(
        functools.partial(project_kernel, n_dp, n_seq, docs),
        out_shape=(
            jax.ShapeDtypeStruct((keys, 2 * LANES), bf16),
            jax.ShapeDtypeStruct((keys, LANES), bf16),
            jax.ShapeDtypeStruct((n_seq, rank, LANES), bf16),
        ),
        in_specs=[vmem] * 6 + [smem] * 2,
        out_specs=(vmem, vmem, vmem),
        scratch_shapes=[
            pltpu.VMEM((rows, LANES), f32),
            pltpu.VMEM((rows, LANES), f32),
            pltpu.VMEM((n_seq, rows, LANES), f32),
            pltpu.VMEM((n_seq, rows, LANES), bf16),
            pltpu.VMEM((rank, rows), f32),
            pltpu.VMEM((rank, rows), bf16),
            pltpu.VMEM((n_seq, rank, rows), bf16),
            pltpu.VMEM((n_seq, rank, LANES), bf16),
            pltpu.SMEM((n_dp,), jnp.int32),
            pltpu.SMEM((n_dp,), jnp.int32),
            pltpu.VMEM((reader.shape[0], img_rows, 3 * LANES), bf16),
            pltpu.VMEM((n_dp, img_rows, 3 * LANES), bf16),
            pltpu.VMEM((n_dp, img_rows, 3 * LANES), bf16),
            dma((n_seq, 4)),
            dma((n_seq, 4)),
            dma((n_seq, 4)),
            dma((n_seq, 4)),
            dma((n_seq,)),
            dma((n_seq,)),
            dma((n_seq,)),
            dma((n_seq,)),
            dma((n_dp,)),
            dma((n_dp,)),
        ],
        compiler_params=pltpu.CompilerParams(
            collective_id=0, has_side_effects=True, vmem_limit_bytes=40 << 20
        ),
    )(tiles, wk, wv, wd, up, gain, reader, doc)


def attend_kernel(
    n_seq,
    docs,
    query_hbm,
    grad_hbm,
    kv_hbm,
    ext_ref,
    up_ref,
    gate_ref,
    length_ref,
    gated_hbm,
    query_grad_hbm,
    small_ref,
    query,
    grad,
    gated,
    query_grad,
    kvs,
    bias,
    load_sem,
    store_sem,
    ring_ss,
    ring_rs,
):
    p = lax.axis_index("dp")
    z = lax.axis_index("seq")
    tokens = query.shape[0]
    rank = up_ref.shape[1]
    keys = ext_ref.shape[0]
    width = query.shape[1] // n_seq
    pair = 2 * LANES
    last = n_seq // 2 - 1
    half = keys // 2
    scale = LANES ** (-0.5)
    right = (p, lax.rem(z + 1, n_seq))
    left = (p, lax.rem(z + n_seq - 1, n_seq))

    def ahead(t, b):
        part = pl.ds(b * half, half)
        source, into = lax.rem(n_seq - t, n_seq), n_seq - 1 - t
        return remote(
            kvs.at[source, part], kvs.at[into, part], ring_ss.at[0, t, b], ring_rs.at[0, t, b], right
        )

    def back(t, b):
        part = pl.ds(b * half, half)
        return remote(
            kvs.at[t, part], kvs.at[t + 1, part], ring_ss.at[1, t, b], ring_rs.at[1, t, b], left
        )

    load_kv = pltpu.make_async_copy(kv_hbm, kvs.at[0], load_sem.at[0])
    load_query = pltpu.make_async_copy(query_hbm, query, load_sem.at[1])
    load_grad = pltpu.make_async_copy(grad_hbm, grad, load_sem.at[2])
    load_kv.start()
    barrier = pltpu.get_barrier_semaphore()
    greet(barrier, right)
    greet(barrier, left)
    load_query.start()
    load_grad.start()
    load_kv.wait()
    pl.semaphore_wait(barrier, 2)
    for b in (0, 1):
        if last > 0 or b == 0:
            ahead(0, b).start()
        if last > 0 or b == 1:
            back(0, b).start()

    lane = lax.broadcasted_iota(jnp.int32, (tokens, LANES), 1)
    place = lax.broadcasted_iota(jnp.int32, (tokens, LANES), 0) + z * tokens
    own_doc = jnp.zeros((tokens, LANES), jnp.int32)
    end = jnp.int32(0)
    for d in range(docs - 1):
        end = end + length_ref[0, d]
        own_doc = own_doc + jnp.where(place >= end, 1, 0)
    other = (lane >= rank) & (lane <= rank + docs) & (lane != rank + own_doc)
    penalty = jnp.where(other, MASKED, 0.0).astype(jnp.bfloat16)
    bias[:tokens, :] = penalty
    bias[tokens:, :] = penalty
    small_ref[...] = jnp.zeros_like(small_ref)
    gate = jnp.tanh(jnp.full((1, LANES), gate_ref[0], jnp.float32))
    load_query.wait()
    load_grad.wait()

    def stack(ref, cols):
        both = ref[:, cols]
        return jnp.concatenate([both[:, :LANES], both[:, LANES:]], axis=0)

    def unstack(x):
        return jnp.concatenate([x[:tokens], x[tokens:]], axis=1)

    def attend_pair(slot, head, j):
        cols = pl.ds(pl.multiple_of(head * width + j * pair, pair), pair)
        own_cols = pl.ds(pl.multiple_of(head * LANES, LANES), LANES)
        q = jnp.concatenate([stack(query, cols), bias[...]], axis=1)
        g = (gate * stack(grad, cols).astype(jnp.float32)).astype(jnp.bfloat16)
        key = kvs[slot, :, :LANES]
        value = kvs[slot, :, LANES:]
        extra = ext_ref[...]
        scores = lax.dot_general(
            q, jnp.concatenate([key, extra], axis=1), NT, preferred_element_type=jnp.float32
        )
        prob_grad = lax.dot_general(g, value, NT, preferred_element_type=jnp.float32)
        row_max = jnp.max(scores, axis=1, keepdims=True)
        weights = jnp.exp2((scores - row_max) * (scale * LOG2_E))
        prob = weights * (1.0 / jnp.sum(weights, axis=1, keepdims=True))
        prob_bf16 = prob.astype(jnp.bfloat16)
        attended = jnp.dot(
            prob_bf16, jnp.concatenate([value, extra], axis=1), preferred_element_type=jnp.float32
        )
        low_seen = attended[:, LANES : LANES + rank].astype(jnp.bfloat16)
        attended = attended[:, :LANES]
        gated[:, cols] = unstack((gate * attended).astype(jnp.bfloat16))
        delta = jnp.sum(g.astype(jnp.float32) * attended, axis=1, keepdims=True)
        score_grad = (prob * (prob_grad - delta)).astype(jnp.bfloat16)
        out_grad = jnp.dot(score_grad, key, preferred_element_type=jnp.float32) * scale
        query_grad[:, cols] = unstack(out_grad.astype(jnp.bfloat16))
        grad_up = lax.dot_general(up_ref[head], g, NT, preferred_element_type=jnp.float32)
        small_ref[:rank, :] += jnp.dot(
            grad_up.astype(jnp.bfloat16), prob_bf16, preferred_element_type=jnp.float32
        )
        small_ref[rank:, own_cols] += lax.dot_general(
            low_seen, g, TN, preferred_element_type=jnp.float32
        )

    def store(i, head):
        cols = pl.ds(pl.multiple_of(head * width, width), width)
        return (
            pltpu.make_async_copy(gated.at[:, cols], gated_hbm.at[:, cols], store_sem.at[0, i]),
            pltpu.make_async_copy(
                query_grad.at[:, cols], query_grad_hbm.at[:, cols], store_sem.at[1, i]
            ),
        )

    def slot_of(i):
        return jnp.where(lax.rem(i, 2) == 1, n_seq - (i + 1) // 2, i // 2)

    def head_step(i):
        step = (i + 1) // 2
        arrives = lax.rem(i, 2) == 1

        @pl.when(arrives & (step <= last))
        def _():
            for b in (0, 1):
                ahead(step - 1, b).wait_recv()
                if b == 0:
                    ahead(step, b).start()
                else:
                    pl.when(step < last)(lambda: ahead(step, 1).start())
                back(step - 1, b).wait_recv()
                if b == 1:
                    back(step, b).start()
                else:
                    pl.when(step < last)(lambda: back(step, 0).start())

        @pl.when(i == n_seq - 1)
        def _():
            ahead(last, 0).wait_recv()
            back(last, 1).wait_recv()

        slot = slot_of(i)
        head = lax.rem(z + slot, n_seq)
        loop(0, width // pair, lambda j: attend_pair(slot, head, j))
        for copy in store(i, head):
            copy.start()

    loop(0, n_seq, head_step)

    def stored(i):
        for copy in store(i, lax.rem(z + slot_of(i), n_seq)):
            copy.wait()

    loop(0, n_seq, stored)
    for t in range(last + 1):
        for b in (0, 1):
            if t < last or b == 0:
                ahead(t, b).wait_send()
            if t < last or b == 1:
                back(t, b).wait_send()


def attend(n_seq, docs, queries, grads, kv, ext, up_all, gate, lengths):
    tokens, columns = queries.shape
    keys = kv.shape[0]
    rank = up_all.shape[1]
    any_space = pl.BlockSpec(memory_space=pl.ANY)
    vmem = pl.BlockSpec(memory_space=pltpu.VMEM)
    smem = pl.BlockSpec(memory_space=pltpu.SMEM)
    f32, bf16, dma = jnp.float32, jnp.bfloat16, pltpu.SemaphoreType.DMA
    wide = pltpu.VMEM((tokens, columns), bf16)
    return pl.pallas_call(
        functools.partial(attend_kernel, n_seq, docs),
        out_shape=(
            jax.ShapeDtypeStruct((tokens, columns), bf16),
            jax.ShapeDtypeStruct((tokens, columns), bf16),
            jax.ShapeDtypeStruct((2 * rank, keys), f32),
        ),
        in_specs=[any_space] * 3 + [vmem] * 2 + [smem] * 2,
        out_specs=(any_space, any_space, vmem),
        scratch_shapes=[
            wide,
            wide,
            wide,
            wide,
            pltpu.VMEM((n_seq, keys, 2 * LANES), bf16),
            pltpu.VMEM((2 * tokens, LANES), bf16),
            dma((3,)),
            dma((2, n_seq)),
            dma((2, n_seq // 2, 2)),
            dma((2, n_seq // 2, 2)),
        ],
        compiler_params=pltpu.CompilerParams(
            collective_id=1, has_side_effects=True, vmem_limit_bytes=48 << 20
        ),
    )(queries, grads, kv, ext, up_all, gate, lengths)


def adapter_kernel(
    n_dp,
    n_seq,
    rank,
    small_ref,
    tiles_ref,
    reader_ref,
    down_ref,
    up_ref,
    col_recv,
    low_send,
    low_recv,
    total,
    sum_recv,
    done,
    col_ss,
    col_rs,
    low_ss,
    low_rs,
    sum_ss,
    sum_rs,
    done_ss,
    done_rs,
):
    p = lax.axis_index("dp")
    z = lax.axis_index("seq")
    rows, width = tiles_ref.shape
    img_dev = reader_ref.shape[0]
    img_rows = rows // img_dev
    fit = LANES // img_rows
    wide = total.shape[1]
    pieces = 2 * (wide // LANES)

    def sends_to(n):
        return fit * z + lax.rem(n, fit), n // fit

    barrier = pltpu.get_barrier_semaphore()
    loop(1, n_seq, lambda k: greet(barrier, (p, lax.rem(z + k, n_seq))))
    loop(1, n_dp, lambda k: greet(barrier, (lax.rem(p + k, n_dp), z)))
    owner = p // fit

    def greet_sender(k):
        g = lax.rem(p + k, n_dp)

        @pl.when((k != 0) | (owner != z))
        def _():
            greet(barrier, (g, owner))

    loop(0, n_dp, greet_sender)
    pl.semaphore_wait(barrier, n_seq - 1 + n_dp - 1 + n_dp - jnp.where(owner == z, 1, 0))

    def col_copy(k):
        target = lax.rem(z + k, n_seq)
        cols = pl.ds(pl.multiple_of(target * LANES, LANES), LANES)
        return remote(
            small_ref.at[:, cols], col_recv.at[k], col_ss.at[k], col_rs.at[k], (p, target)
        )

    loop(1, n_seq, lambda k: col_copy(k).start())
    own = small_ref[:, pl.ds(pl.multiple_of(z * LANES, LANES), LANES)]
    for k in range(1, n_seq):
        col_copy(k).wait_recv()
        own = own + col_recv[k]
    own = ADAPTER_SCALE * own
    low_send[...] = own[:rank].astype(jnp.bfloat16)
    total[:, width:] = jnp.zeros((rank, wide - width), jnp.float32)
    total[:, wide - LANES :] = own[rank:]

    def low_copy(n, slot):
        o, s = sends_to(n)
        return remote(low_send, low_recv.at[slot], low_ss.at[n], low_rs.at[p], (o, s))

    def low_start(n):
        o, s = sends_to(n)
        mine = (o == p) & (s == z)

        @pl.when(mine)
        def _():
            low_recv[p] = low_send[...]

        @pl.when(jnp.logical_not(mine))
        def _():
            low_copy(n, p).start()

    loop(0, fit * n_seq, low_start)

    def low_wait(g):
        @pl.when((g != p) | (owner != z))
        def _():
            remote(
                low_send, low_recv.at[g], low_ss.at[0], low_rs.at[g], (g, owner)
            ).wait_recv()

    loop(0, n_dp, low_wait)

    lane = lax.broadcasted_iota(jnp.int32, (rank, LANES), 1)
    held = lax.rem(p, fit)
    for first in range(0, img_dev, fit):
        piece = jnp.zeros((rank, LANES), jnp.float32)
        for i in range(fit):
            block = low_recv[reader_ref[first + i]].astype(jnp.float32)
            shift = lax.rem(i - held + fit, fit) * img_rows
            block = pltpu.roll(block, shift, 1)
            piece = jnp.where(lane // img_rows == i, block, piece)
        part = jnp.dot(
            piece.astype(jnp.bfloat16),
            tiles_ref[first * img_rows : (first + fit) * img_rows, :],
            preferred_element_type=jnp.float32,
        )
        if first == 0:
            total[:, :width] = part
        else:
            total[:, :width] += part

    def piece_of(ref, j):
        return ref.at[
            pl.ds(pl.multiple_of(lax.rem(j, 2) * 8, 8), 8),
            pl.ds(pl.multiple_of((j // 2) * LANES, LANES), LANES),
        ]

    def sum_copy(j):
        k = lax.rem(j - p + n_dp, n_dp)
        return remote(
            piece_of(total, j), sum_recv.at[k], sum_ss.at[j], sum_rs.at[k], (j, z)
        )

    loop(0, pieces, lambda j: pl.when(j != p)(lambda: sum_copy(j).start()))

    def done_copy(k, j):
        g = lax.rem(p + k, n_dp)
        return remote(done.at[j], done.at[j], done_ss.at[k], done_rs.at[j], (g, z))

    @pl.when(p < pieces)
    def _():
        def take(k, acc):
            remote(
                piece_of(total, p), sum_recv.at[k], sum_ss.at[0], sum_rs.at[k], (p, z)
            ).wait_recv()
            return acc + sum_recv[k]

        done[p] = lax.fori_loop(1, n_dp, take, piece_of(total, p)[...])
        loop(1, n_dp, lambda k: done_copy(k, p).start())

    loop(0, pieces, lambda j: pl.when(j != p)(lambda: done_copy(0, j).wait_recv()))
    for j in range(pieces - 2):
        r, c = 8 * (j % 2), LANES * (j // 2)
        fill = min(LANES, width - c)
        if fill > 0:
            down_ref[r : r + 8, c : c + fill] = done[j][:, :fill]
    up_ref[:8, :] = done[pieces - 2]
    up_ref[8:, :] = done[pieces - 1]

    loop(1, n_seq, lambda k: col_copy(k).wait_send())

    def low_sent(n):
        o, s = sends_to(n)

        @pl.when((o != p) | (s != z))
        def _():
            low_copy(n, p).wait_send()

    loop(0, fit * n_seq, low_sent)
    loop(0, pieces, lambda j: pl.when(j != p)(lambda: sum_copy(j).wait_send()))

    @pl.when(p < pieces)
    def _():
        loop(1, n_dp, lambda k: done_copy(k, p).wait_send())


def adapter(n_dp, n_seq, rank, small, tiles, reader):
    rows, width = tiles.shape
    wide = -(-width // LANES) * LANES + LANES
    pieces = 2 * (wide // LANES)
    img_rows = rows // reader.shape[0]
    vmem = pl.BlockSpec(memory_space=pltpu.VMEM)
    smem = pl.BlockSpec(memory_space=pltpu.SMEM)
    f32, bf16, dma = jnp.float32, jnp.bfloat16, pltpu.SemaphoreType.DMA
    fan = (LANES // img_rows) * n_seq
    return pl.pallas_call(
        functools.partial(adapter_kernel, n_dp, n_seq, rank),
        out_shape=(
            jax.ShapeDtypeStruct((rank, width), f32),
            jax.ShapeDtypeStruct((rank, LANES), f32),
        ),
        in_specs=[vmem, vmem, smem],
        out_specs=(vmem, vmem),
        scratch_shapes=[
            pltpu.VMEM((n_seq, 2 * rank, LANES), f32),
            pltpu.VMEM((rank, LANES), bf16),
            pltpu.VMEM((n_dp, rank, LANES), bf16),
            pltpu.VMEM((rank, wide), f32),
            pltpu.VMEM((n_dp, 8, LANES), f32),
            pltpu.VMEM((pieces, 8, LANES), f32),
            dma((n_seq,)),
            dma((n_seq,)),
            dma((fan,)),
            dma((n_dp,)),
            dma((pieces,)),
            dma((n_dp,)),
            dma((n_dp,)),
            dma((pieces,)),
        ],
        compiler_params=pltpu.CompilerParams(
            collective_id=2, has_side_effects=True, vmem_limit_bytes=16 << 20
        ),
    )(small, tiles, reader)


def per_device(
    queries,
    output_gradient,
    tiles,
    frozen_key_weight,
    frozen_value_weight,
    key_norm_gain,
    adapter_down_weight,
    adapter_up_weight,
    gate,
    document_lengths,
    image_reader_group,
    image_document,
):
    n_dp, n_seq = lax.axis_size("dp"), lax.axis_size("seq")
    docs = document_lengths.shape[1]
    rank = adapter_up_weight.shape[0]
    img_dev, img_rows, width = tiles.shape
    flat_tiles = tiles.reshape(img_dev * img_rows, width)
    kv, ext, up_all = project(
        n_dp,
        n_seq,
        docs,
        flat_tiles,
        frozen_key_weight,
        frozen_value_weight,
        adapter_down_weight,
        adapter_up_weight,
        key_norm_gain.reshape(1, -1),
        image_reader_group,
        image_document,
    )
    gated, query_grad, small = attend(
        n_seq, docs, queries, output_gradient, kv, ext, up_all, gate, document_lengths
    )
    down_rows, up_grad = adapter(n_dp, n_seq, rank, small, flat_tiles, image_reader_group)
    return (gated, query_grad, down_rows.T, up_grad)


def solution(mesh):
    placed = (
        P(("dp", "seq"), None),
        P(("dp", "seq"), None),
        P("dp", None, "seq"),
        P("seq", None),
        P("seq", None),
        P(),
        P("seq", None),
        P(None, "seq"),
        P(),
        P("dp", None),
        P("dp"),
        P("dp"),
    )
    return jax.shard_map(
        per_device,
        mesh=mesh,
        in_specs=placed,
        out_specs=(P(("dp", "seq"), None), P(("dp", "seq"), None), P("seq", None), P(None, "seq")),
        check_vma=False,
    )
```

```python
import functools

import jax
import jax.numpy as jnp
from jax import lax
from jax.experimental import pallas as pl
from jax.experimental.pallas import tpu as pltpu
from jax.sharding import PartitionSpec as P

EPS = 1e-05
ADAPTER_SCALE = 2.0
MASKED = -1e30
LANES = 128
CHUNK = 64
PARTS = 4
HEADS_AT_ONCE = 4
LOG2_E = 1.4426950408889634
MESH = pl.DeviceIdType.MESH
NT = (((1,), (1,)), ((), ()))
TN = (((0,), (0,)), ((), ()))


def remote(src, dst, send_sem, recv_sem, target):
    return pltpu.make_async_remote_copy(
        src_ref=src,
        dst_ref=dst,
        send_sem=send_sem,
        recv_sem=recv_sem,
        device_id=target,
        device_id_type=MESH,
    )


def loop(first, last, body):
    def step(i, carry):
        body(i)
        return carry

    lax.fori_loop(first, last, step, 0)


def greet(barrier, target):
    pl.semaphore_signal(barrier, inc=1, device_id=target, device_id_type=MESH)


def fused_kernel(
    n_dp,
    n_seq,
    docs,
    query_hbm,
    grad_hbm,
    tiles_hbm,
    wk_hbm,
    wv_hbm,
    wd_hbm,
    up_ref,
    gain_ref,
    gate_ref,
    length_ref,
    reader_ref,
    doc_ref,
    gated_hbm,
    query_grad_hbm,
    down_ref,
    up_out_ref,
    query,
    grad,
    gated,
    query_grad,
    tiles,
    wk,
    wv,
    wd,
    own_k,
    own_v,
    sum_k,
    sum_v,
    low_own,
    low_out,
    low_in,
    up_all,
    pick,
    tag,
    rows_buf,
    ext_rows,
    kv_out,
    ext_out,
    kvs,
    ext,
    bias,
    prob_buf,
    delta_buf,
    small,
    col_in,
    back_out,
    back_in,
    total,
    sum_in,
    done,
    load_sem,
    store_sem,
    k_ss,
    k_rs,
    v_ss,
    v_rs,
    low_ss,
    low_rs,
    up_ss,
    up_rs,
    kv_ss,
    kv_rs,
    ext_ss,
    ext_rs,
    ring_ss,
    ring_rs,
    col_ss,
    col_rs,
    back_ss,
    back_rs,
    sum_ss,
    sum_rs,
    done_ss,
    done_rs,
):
    p = lax.axis_index("dp")
    z = lax.axis_index("seq")
    rows, width = tiles.shape
    tokens, columns = query.shape
    rank = up_ref.shape[0]
    img_dev = reader_ref.shape[0]
    img_rows = rows // img_dev
    keys = ext.shape[0]
    head_width = columns // n_seq
    block = bias.shape[0]
    fit = LANES // img_rows
    half = rows // 2
    chunks = rows // CHUNK
    scale = LANES ** (-0.5)
    right = (p, lax.rem(z + 1, n_seq))
    left = (p, lax.rem(z + n_seq - 1, n_seq))

    def lanes_of(n, size=LANES):
        return pl.ds(pl.multiple_of(n * size, size), size)

    loads = [
        pltpu.make_async_copy(source, into, load_sem.at[n])
        for n, (source, into) in enumerate(
            (
                (tiles_hbm, tiles),
                (wk_hbm, wk),
                (wv_hbm, wv),
                (wd_hbm, wd),
                (query_hbm, query),
                (grad_hbm, grad),
            )
        )
    ]
    for load in loads:
        load.start()
    barrier = pltpu.get_barrier_semaphore()
    loop(1, n_seq, lambda k: greet(barrier, (p, lax.rem(z + k, n_seq))))
    loop(1, n_dp, lambda k: greet(barrier, (lax.rem(p + k, n_dp), z)))

    def greet_back(k):
        @pl.when((k != 0) | (z != 0))
        def _():
            greet(barrier, (lax.rem(p + k, n_dp), k // fit))

    loop(0, n_dp, greet_back)

    def own_part(t):
        ahead = lax.rem(z + 2 * n_seq - 1 - t, n_seq)
        back = lax.rem(z + 1 + t, n_seq)
        for side, head in ((0, ahead), (1, back)):
            part = pl.ds(side * half, half)
            x = tiles[part, :]
            own_k[part, :] = jnp.dot(x, wk[:, lanes_of(head)], preferred_element_type=jnp.float32)
            own_v[part, :] = jnp.dot(x, wv[:, lanes_of(head)], preferred_element_type=jnp.float32)

    order = [c + side * (chunks // 2) for c in range(chunks // 2) for side in (0, 1)]

    def hop(t, s):
        target = right if s < chunks // 2 else left
        part = pl.ds(s * CHUNK, CHUNK)
        return (
            remote(sum_k.at[t, part], sum_k.at[t + 1, part], k_ss.at[t, s], k_rs.at[t, s], target),
            remote(sum_v.at[t, part], sum_v.at[t + 1, part], v_ss.at[t, s], v_rs.at[t, s], target),
        )

    for load in loads[:3]:
        load.wait()
    own_part(0)
    sum_k[0] = own_k[...]
    sum_v[0] = own_v[...].astype(jnp.bfloat16)
    pl.semaphore_wait(barrier, n_seq - 1 + n_dp - 1 + n_dp - jnp.where(z == 0, 1, 0))
    for s in order:
        for copy in hop(0, s):
            copy.start()

    def low_copy(k):
        target = (p, lax.rem(z + k, n_seq))
        return remote(low_out, low_in.at[k], low_ss.at[k], low_rs.at[k], target)

    def up_copy(k, slot):
        target = (p, lax.rem(z + k, n_seq))
        return remote(up_ref, up_all.at[slot], up_ss.at[k], up_rs.at[k], target)

    loads[3].wait()
    low_own[...] = lax.dot_general(wd[...], tiles[...], NT, preferred_element_type=jnp.float32)
    low_out[...] = low_own[...].astype(jnp.bfloat16)
    loop(1, n_seq, lambda k: low_copy(k).start())
    loop(1, n_seq, lambda k: up_copy(k, z).start())
    up_all[z] = up_ref[...]

    def find(g):
        at, mark = jnp.int32(0), jnp.int32(docs)
        for i in range(img_dev):
            hit = reader_ref[i] == g
            at = jnp.where(hit, i, at)
            mark = jnp.where(hit, doc_ref[i], mark)
        pick[g] = at
        tag[g] = mark

    def kv_copy(k):
        g = lax.rem(p + k, n_dp)
        into = kvs.at[0, pl.ds(pl.multiple_of(k * img_rows, img_rows), img_rows)]
        return remote(kv_out.at[k], into, kv_ss.at[k], kv_rs.at[k], (g, z))

    def ext_copy(k):
        g = lax.rem(p + k, n_dp)
        into = ext.at[pl.ds(pl.multiple_of(k * img_rows, img_rows), img_rows)]
        return remote(ext_out.at[k], into, ext_ss.at[k], ext_rs.at[k], (g, z))

    lane = lax.broadcasted_iota(jnp.int32, (img_rows, LANES), 1)

    def ext_block(g):
        mark = jnp.where(lane == rank + tag[g], 1.0, 0.0)
        low = ext_rows[pick[g]].astype(jnp.float32)
        return jnp.where(lane < rank, low, mark).astype(jnp.bfloat16)

    def send_ext(k):
        ext_out[k] = ext_block(lax.rem(p + k, n_dp))
        ext_copy(k).start()

    def low_finish():
        low_total = low_own[...]
        for k in range(1, n_seq):
            low_copy(k).wait_recv()
            low_total = low_total + low_in[k].astype(jnp.float32)
        low_rank = low_total.astype(jnp.bfloat16)
        low_out[...] = low_rank
        eye = lax.broadcasted_iota(jnp.int32, (rank, LANES), 0) == lax.broadcasted_iota(
            jnp.int32, (rank, LANES), 1
        )
        eye = jnp.where(eye, 1.0, 0.0).astype(jnp.bfloat16)
        low_rows = lax.dot_general(low_rank, eye, TN, preferred_element_type=jnp.float32)
        ext_rows[...] = low_rows.astype(jnp.bfloat16).reshape(img_dev, img_rows, LANES)

    def low_sends():
        loop(1, n_seq, lambda k: low_copy(k).wait_send())

    def ring_step(t):
        own_part(t)
        for s in order:
            part = pl.ds(s * CHUNK, CHUNK)
            for copy in hop(t - 1, s):
                copy.wait_recv()
            sum_k[t, part, :] = sum_k[t, part, :] + own_k[part, :]
            total_v = sum_v[t, part, :].astype(jnp.float32) + own_v[part, :]
            sum_v[t, part, :] = total_v.astype(jnp.bfloat16)
            for copy in hop(t, s):
                copy.start()

    if n_seq > 3:
        loop(0, n_dp, find)
        loop(1, 3, ring_step)
        low_sends()
        low_finish()
        each = -(-(n_dp - 1) // (n_seq - 4))

        def ring_and_ext(t):
            first = 1 + (t - 3) * each
            loop(first, jnp.minimum(first + each, n_dp), send_ext)
            ring_step(t)

        loop(3, n_seq - 1, ring_and_ext)
    else:
        loop(0, n_dp, find)
        loop(1, n_seq - 1, ring_step)
        low_sends()
        low_finish()
        loop(1, n_dp, send_ext)
    ext[:img_rows, :] = ext_block(p)

    own_part(n_seq - 1)
    low_up = lax.dot_general(low_out[...], up_ref[...], TN, preferred_element_type=jnp.float32)
    own_v[...] = own_v[...] + ADAPTER_SCALE * low_up

    lane_tok = lax.broadcasted_iota(jnp.int32, (tokens, LANES), 1)
    place = lax.broadcasted_iota(jnp.int32, (tokens, LANES), 0) + z * tokens
    own_doc = jnp.zeros((tokens, LANES), jnp.int32)
    end = jnp.int32(0)
    for d in range(docs - 1):
        end = end + length_ref[0, d]
        own_doc = own_doc + jnp.where(place >= end, 1, 0)
    other = (lane_tok >= rank) & (lane_tok <= rank + docs) & (lane_tok != rank + own_doc)
    penalty = jnp.where(other, MASKED, 0.0).astype(jnp.bfloat16)
    for n in range(block // tokens):
        bias[n * tokens : (n + 1) * tokens, :] = penalty
    small[...] = jnp.zeros_like(small)
    gate = jnp.tanh(jnp.full((1, LANES), gate_ref[0], jnp.float32))

    per_chunk = CHUNK // img_rows
    for s in order:
        part = pl.ds(s * CHUNK, CHUNK)
        images = pl.ds(s * per_chunk, per_chunk)
        for copy in hop(n_seq - 2, s):
            copy.wait_recv()
        key_raw = sum_k[n_seq - 1, part, :] + own_k[part, :]
        mean_square = jnp.mean(key_raw * key_raw, axis=-1, keepdims=True)
        key_rows = key_raw * lax.rsqrt(mean_square + EPS) * gain_ref[...]
        value = sum_v[n_seq - 1, part, :].astype(jnp.float32) + own_v[part, :]
        both = jnp.concatenate([key_rows, value], axis=1).astype(jnp.bfloat16)
        rows_buf[images] = both.reshape(per_chunk, img_rows, 2 * LANES)

    def send_kv(k):
        kv_out[k] = rows_buf[pick[lax.rem(p + k, n_dp)]]
        kv_copy(k).start()

    loop(1, n_dp, send_kv)
    kvs[0, :img_rows, :] = rows_buf[pick[p]]

    last = n_seq // 2 - 1
    part_rows = keys // PARTS

    def ahead(t, b):
        part = pl.ds(b * part_rows, part_rows)
        source, into = lax.rem(n_seq - t, n_seq), n_seq - 1 - t
        return remote(
            kvs.at[source, part], kvs.at[into, part], ring_ss.at[0, t, b], ring_rs.at[0, t, b], right
        )

    def back(t, b):
        part = pl.ds(b * part_rows, part_rows)
        return remote(
            kvs.at[t, part], kvs.at[t + 1, part], ring_ss.at[1, t, b], ring_rs.at[1, t, b], left
        )

    ways = ((ahead, lambda b: b < PARTS // 2), (back, lambda b: b >= PARTS // 2))
    slots = n_dp // PARTS
    for b in range(PARTS):
        loop(max(1, b * slots), (b + 1) * slots, lambda k: kv_copy(k).wait_recv())
        for way, whole in ways:
            if last > 0 or whole(b):
                way(0, b).start()
    loop(1, n_dp, lambda k: ext_copy(k).wait_recv())
    loop(1, n_seq, lambda k: up_copy(k, lax.rem(z + n_seq - k, n_seq)).wait_recv())
    loads[4].wait()
    loads[5].wait()

    def stack(ref, cols):
        part = ref[:, cols]
        return jnp.concatenate(
            [part[:, n * LANES : (n + 1) * LANES] for n in range(block // tokens)], axis=0
        )

    def unstack(x):
        return jnp.concatenate(
            [x[n * tokens : (n + 1) * tokens] for n in range(block // tokens)], axis=1
        )

    span = (block // tokens) * LANES

    def cols_of(head, j):
        return pl.ds(pl.multiple_of(head * head_width + j * span, span), span)

    def grad_rows(cols):
        return (gate * stack(grad, cols).astype(jnp.float32)).astype(jnp.bfloat16)

    def probabilities(slot, head, j):
        cols = cols_of(head, j)
        q = jnp.concatenate([stack(query, cols), bias[...]], axis=1)
        g = grad_rows(cols)
        key_ext = jnp.concatenate([kvs[slot, :, :LANES], ext[...]], axis=1)
        scores = lax.dot_general(q, key_ext, NT, preferred_element_type=jnp.float32)
        row_max = jnp.max(scores, axis=1, keepdims=True)
        weights = jnp.exp2((scores - row_max) * (scale * LOG2_E))
        prob = weights * (1.0 / jnp.sum(weights, axis=1, keepdims=True))
        prob_bf16 = prob.astype(jnp.bfloat16)
        value_ext = jnp.concatenate([kvs[slot, :, LANES:], ext[...]], axis=1)
        attended = jnp.dot(prob_bf16, value_ext, preferred_element_type=jnp.float32)
        low_seen = attended[:, LANES : LANES + rank].astype(jnp.bfloat16)
        attended = attended[:, :LANES]
        gated[:, cols] = unstack((gate * attended).astype(jnp.bfloat16))
        delta = jnp.sum(g.astype(jnp.float32) * attended, axis=1, keepdims=True)
        grad_up = lax.dot_general(up_all[head], g, NT, preferred_element_type=jnp.float32)
        small[:rank, :] += jnp.dot(
            grad_up.astype(jnp.bfloat16), prob_bf16, preferred_element_type=jnp.float32
        )
        small[rank:, lanes_of(head)] += lax.dot_general(
            low_seen, g, TN, preferred_element_type=jnp.float32
        )
        return g, prob, delta

    def query_gradient(slot, head, j, g, prob, delta):
        prob_grad = lax.dot_general(
            g, kvs[slot, :, LANES:], NT, preferred_element_type=jnp.float32
        )
        score_grad = (prob * (prob_grad - delta)).astype(jnp.bfloat16)
        out_grad = jnp.dot(score_grad, kvs[slot, :, :LANES], preferred_element_type=jnp.float32)
        query_grad[:, cols_of(head, j)] = unstack((out_grad * scale).astype(jnp.bfloat16))

    def store(n, i, head):
        cols = lanes_of(head, head_width)
        source, into = ((gated, gated_hbm), (query_grad, query_grad_hbm))[n]
        return pltpu.make_async_copy(source.at[:, cols], into.at[:, cols], store_sem.at[n, i])

    def slot_of(i):
        return jnp.where(lax.rem(i, 2) == 1, n_seq - (i + 1) // 2, i // 2)

    blocks = head_width // span

    def head_step(i):
        step = (i + 1) // 2

        @pl.when((lax.rem(i, 2) == 1) & (step <= last))
        def _():
            for b in range(PARTS):
                for way, whole in ways:
                    way(step - 1, b).wait_recv()
                    if whole(b):
                        way(step, b).start()
                    else:
                        pl.when(step < last)(lambda: way(step, b).start())

        slot = slot_of(i)
        head = lax.rem(z + slot, n_seq)

        def both(j):
            query_gradient(slot, head, j, *probabilities(slot, head, j))

        loop(0, blocks, both)
        store(0, i, head).start()
        store(1, i, head).start()

    loop(0, n_seq - 1, head_step)
    for b in range(PARTS):
        for way, whole in ways:
            if whole(b):
                way(last, b).wait_recv()
    far = n_seq // 2
    far_head = lax.rem(z + far, n_seq)

    def far_first(j):
        unused, prob, delta = probabilities(far, far_head, j)
        prob_buf[j] = prob
        delta_buf[j] = jnp.broadcast_to(delta, (block, LANES))

    def far_second(j):
        g = grad_rows(cols_of(far_head, j))
        query_gradient(far, far_head, j, g, prob_buf[j], delta_buf[j][:, :1])

    loop(0, blocks, far_first)
    store(0, n_seq - 1, far_head).start()

    def col_copy(k):
        target = lax.rem(z + k, n_seq)
        return remote(
            small.at[:, lanes_of(target)], col_in.at[k], col_ss.at[k], col_rs.at[k], (p, target)
        )

    loop(1, n_seq, lambda k: col_copy(k).start())
    loop(0, blocks, far_second)
    store(1, n_seq - 1, far_head).start()
    own = small[:, lanes_of(z)]
    for k in range(1, n_seq):
        col_copy(k).wait_recv()
        own = own + col_in[k]
    own = ADAPTER_SCALE * own
    for j in range(fit):
        moved = own[:rank]
        if j > 0:
            moved = pltpu.roll(moved, LANES - j * img_rows, 1)
        back_out[j] = moved.astype(jnp.bfloat16)
    wide = total.shape[1]
    pieces = 2 * (wide // LANES)
    total[:, width:] = jnp.zeros((rank, wide - width), jnp.float32)
    total[:, wide - LANES :] = own[rank:]

    def back_copy(n):
        j, s = lax.rem(n, fit), n // fit
        o = lax.rem(p + n_dp - fit * z - j, n_dp)
        return remote(back_out.at[j], back_in.at[p], back_ss.at[n], back_rs.at[p], (o, s))

    def unless_own(n, act):
        pl.when((n != 0) | (z != 0))(act)

    loop(0, fit * n_seq, lambda n: unless_own(n, lambda: back_copy(n).start()))

    @pl.when(z == 0)
    def _():
        back_in[p] = back_out[0]

    def back_wait(k):
        g = lax.rem(p + k, n_dp)
        copy = remote(
            back_out.at[0], back_in.at[g], back_ss.at[0], back_rs.at[g], (g, k // fit)
        )
        unless_own(k, lambda: copy.wait_recv())

    loop(0, n_dp, back_wait)

    lane_rank = lax.broadcasted_iota(jnp.int32, (rank, LANES), 1)
    pieces_in = []
    for first in range(0, img_dev, fit):
        piece = jnp.zeros((rank, LANES), jnp.float32)
        for i in range(fit):
            held = back_in[reader_ref[first + i]].astype(jnp.float32)
            if i > 0:
                held = pltpu.roll(held, i * img_rows, 1)
            piece = jnp.where(lane_rank // img_rows == i, held, piece)
        pieces_in.append(piece.astype(jnp.bfloat16))
    total[:, :width] = jnp.dot(
        jnp.concatenate(pieces_in, axis=1), tiles[...], preferred_element_type=jnp.float32
    )

    def piece_of(j):
        return total.at[
            pl.ds(pl.multiple_of(lax.rem(j, 2) * 8, 8), 8),
            lanes_of(j // 2),
        ]

    def sum_copy(j):
        k = lax.rem(j - p + n_dp, n_dp)
        return remote(piece_of(j), sum_in.at[k], sum_ss.at[j], sum_rs.at[k], (j, z))

    loop(0, pieces, lambda j: pl.when(j != p)(lambda: sum_copy(j).start()))

    def done_copy(k, j):
        g = lax.rem(p + k, n_dp)
        return remote(done.at[j], done.at[j], done_ss.at[k], done_rs.at[j], (g, z))

    @pl.when(p < pieces)
    def _():
        def take(k, acc):
            remote(
                piece_of(p), sum_in.at[k], sum_ss.at[0], sum_rs.at[k], (p, z)
            ).wait_recv()
            return acc + sum_in[k]

        done[p] = lax.fori_loop(1, n_dp, take, piece_of(p)[...])
        loop(1, n_dp, lambda k: done_copy(k, p).start())

    def ring_sent(t):
        for s in range(chunks):
            for copy in hop(t, s):
                copy.wait_send()

    loop(0, n_seq - 1, ring_sent)
    loop(1, n_seq, lambda k: up_copy(k, z).wait_send())
    loop(1, n_dp, lambda k: kv_copy(k).wait_send())
    loop(1, n_dp, lambda k: ext_copy(k).wait_send())
    for t in range(last + 1):
        for b in range(PARTS):
            for way, whole in ways:
                if t < last or whole(b):
                    way(t, b).wait_send()
    loop(1, n_seq, lambda k: col_copy(k).wait_send())
    loop(0, fit * n_seq, lambda n: unless_own(n, lambda: back_copy(n).wait_send()))
    loop(0, pieces, lambda j: pl.when(j != p)(lambda: sum_copy(j).wait_send()))

    def stored(i):
        head = lax.rem(z + slot_of(i), n_seq)
        store(0, i, head).wait()
        store(1, i, head).wait()

    loop(0, n_seq, stored)

    loop(0, pieces, lambda j: pl.when(j != p)(lambda: done_copy(0, j).wait_recv()))
    for j in range(pieces - 2):
        r, c = 8 * (j % 2), LANES * (j // 2)
        fill = min(LANES, width - c)
        if fill > 0:
            down_ref[r : r + 8, c : c + fill] = done[j][:, :fill]
    up_out_ref[:8, :] = done[pieces - 2]
    up_out_ref[8:, :] = done[pieces - 1]

    @pl.when(p < pieces)
    def _():
        loop(1, n_dp, lambda k: done_copy(k, p).wait_send())


def per_device(
    queries,
    output_gradient,
    tiles,
    frozen_key_weight,
    frozen_value_weight,
    key_norm_gain,
    adapter_down_weight,
    adapter_up_weight,
    gate,
    document_lengths,
    image_reader_group,
    image_document,
):
    n_dp, n_seq = lax.axis_size("dp"), lax.axis_size("seq")
    docs = document_lengths.shape[1]
    rank = adapter_up_weight.shape[0]
    img_dev, img_rows, width = tiles.shape
    rows = img_dev * img_rows
    tokens, columns = queries.shape
    keys = n_dp * img_rows
    block = min(HEADS_AT_ONCE * LANES, columns // n_seq) // LANES * tokens
    blocks = (columns // n_seq) // LANES * tokens // block
    wide = -(-width // LANES) * LANES + LANES
    pieces = 2 * (wide // LANES)
    fan = (LANES // img_rows) * n_seq
    chunks = rows // CHUNK
    any_space = pl.BlockSpec(memory_space=pl.ANY)
    vmem = pl.BlockSpec(memory_space=pltpu.VMEM)
    smem = pl.BlockSpec(memory_space=pltpu.SMEM)
    f32, bf16 = jnp.float32, jnp.bfloat16

    def held(*shape, kind=bf16):
        return pltpu.VMEM(shape, kind)

    dma = pltpu.SemaphoreType.DMA
    gated, query_grad, down_rows, up_grad = pl.pallas_call(
        functools.partial(fused_kernel, n_dp, n_seq, docs),
        out_shape=(
            jax.ShapeDtypeStruct((tokens, columns), bf16),
            jax.ShapeDtypeStruct((tokens, columns), bf16),
            jax.ShapeDtypeStruct((rank, width), f32),
            jax.ShapeDtypeStruct((rank, LANES), f32),
        ),
        in_specs=[any_space] * 6 + [vmem] * 2 + [smem] * 4,
        out_specs=(any_space, any_space, vmem, vmem),
        scratch_shapes=[
            held(tokens, columns),
            held(tokens, columns),
            held(tokens, columns),
            held(tokens, columns),
            held(rows, width),
            held(width, n_seq * LANES),
            held(width, n_seq * LANES),
            held(rank, width),
            held(rows, LANES, kind=f32),
            held(rows, LANES, kind=f32),
            held(n_seq, rows, LANES, kind=f32),
            held(n_seq, rows, LANES),
            held(rank, rows, kind=f32),
            held(rank, rows),
            held(n_seq, rank, rows),
            held(n_seq, rank, LANES),
            pltpu.SMEM((n_dp,), jnp.int32),
            pltpu.SMEM((n_dp,), jnp.int32),
            held(img_dev, img_rows, 2 * LANES),
            held(img_dev, img_rows, LANES),
            held(n_dp, img_rows, 2 * LANES),
            held(n_dp, img_rows, LANES),
            held(n_seq, keys, 2 * LANES),
            held(keys, LANES),
            held(block, LANES),
            held(blocks, block, keys, kind=f32),
            held(blocks, block, LANES, kind=f32),
            held(2 * rank, keys, kind=f32),
            held(n_seq, 2 * rank, LANES, kind=f32),
            held(LANES // img_rows, rank, LANES),
            held(n_dp, rank, LANES),
            held(rank, wide, kind=f32),
            held(n_dp, 8, LANES, kind=f32),
            held(pieces, 8, LANES, kind=f32),
            dma((6,)),
            dma((2, n_seq)),
            dma((n_seq, chunks)),
            dma((n_seq, chunks)),
            dma((n_seq, chunks)),
            dma((n_seq, chunks)),
            dma((n_seq,)),
            dma((n_seq,)),
            dma((n_seq,)),
            dma((n_seq,)),
            dma((n_dp,)),
            dma((n_dp,)),
            dma((n_dp,)),
            dma((n_dp,)),
            dma((2, n_seq // 2, PARTS)),
            dma((2, n_seq // 2, PARTS)),
            dma((n_seq,)),
            dma((n_seq,)),
            dma((fan,)),
            dma((n_dp,)),
            dma((pieces,)),
            dma((n_dp,)),
            dma((n_dp,)),
            dma((pieces,)),
        ],
        compiler_params=pltpu.CompilerParams(
            collective_id=0, has_side_effects=True, vmem_limit_bytes=58 << 20
        ),
    )(
        queries,
        output_gradient,
        tiles.reshape(rows, width),
        frozen_key_weight,
        frozen_value_weight,
        adapter_down_weight.T,
        adapter_up_weight,
        key_norm_gain.reshape(1, -1),
        gate,
        document_lengths,
        image_reader_group,
        image_document,
    )
    return (gated, query_grad, down_rows.T, up_grad)


def solution(mesh):
    placed = (
        P(("dp", "seq"), None),
        P(("dp", "seq"), None),
        P("dp", None, "seq"),
        P("seq", None),
        P("seq", None),
        P(),
        P("seq", None),
        P(None, "seq"),
        P(),
        P("dp", None),
        P("dp"),
        P("dp"),
    )
    return jax.shard_map(
        per_device,
        mesh=mesh,
        in_specs=placed,
        out_specs=(P(("dp", "seq"), None), P(("dp", "seq"), None), P("seq", None), P(None, "seq")),
        check_vma=False,
    )
```

```python
import functools

import jax
import jax.numpy as jnp
from jax import lax
from jax.experimental import pallas as pl
from jax.experimental.pallas import tpu as pltpu
from jax.sharding import PartitionSpec as P

EPS = 1e-05
ADAPTER_SCALE = 2.0
MASKED = -1e30
LANES = 128
CHUNK = 64
PARTS = 4
HEADS_AT_ONCE = 4
LAG = 2
LOG2_E = 1.4426950408889634
MESH = pl.DeviceIdType.MESH
NT = (((1,), (1,)), ((), ()))
TN = (((0,), (0,)), ((), ()))


def remote(src, dst, send_sem, recv_sem, target):
    return pltpu.make_async_remote_copy(
        src_ref=src,
        dst_ref=dst,
        send_sem=send_sem,
        recv_sem=recv_sem,
        device_id=target,
        device_id_type=MESH,
    )


def loop(first, last, body):
    def step(i, carry):
        body(i)
        return carry

    lax.fori_loop(first, last, step, 0)


def greet(barrier, target):
    pl.semaphore_signal(barrier, inc=1, device_id=target, device_id_type=MESH)


def fused_kernel(
    n_dp,
    n_seq,
    docs,
    query_hbm,
    grad_hbm,
    tiles_hbm,
    wk_hbm,
    wv_hbm,
    wd_hbm,
    up_hbm,
    gain_hbm,
    gate_hbm,
    length_hbm,
    reader_hbm,
    doc_hbm,
    gated_hbm,
    query_grad_hbm,
    down_hbm,
    up_out_hbm,
    query,
    grad,
    gated,
    query_grad,
    tiles,
    wk,
    wv,
    wd,
    up,
    gain,
    gate_s,
    lengths,
    reader,
    doc,
    own_k,
    own_v,
    sum_k,
    sum_v,
    low_own,
    low_out,
    low_in,
    up_all,
    pick,
    tag,
    rows_k,
    rows_v,
    ext_rows,
    k_out,
    v_out,
    ext_out,
    k_all,
    v_all,
    ext,
    ext_t,
    bias,
    probs,
    value_grad,
    small,
    col_in,
    back_out,
    back_in,
    total,
    sum_in,
    done,
    down_stage,
    up_stage,
    load_sem,
    store_sem,
    out_sem,
    k_ss,
    k_rs,
    v_ss,
    v_rs,
    low_ss,
    low_rs,
    up_ss,
    up_rs,
    route_ss,
    route_rs,
    ring_ss,
    ring_rs,
    col_ss,
    col_rs,
    back_ss,
    back_rs,
    sum_ss,
    sum_rs,
    done_ss,
    done_rs,
):
    p = lax.axis_index("dp")
    z = lax.axis_index("seq")
    rows, width = tiles.shape
    tokens, columns = query.shape
    rank = up.shape[0]
    img_dev, img_rows = rows_k.shape[:2]
    keys = ext.shape[0]
    head_width = columns // n_seq
    block = bias.shape[0]
    span = (block // tokens) * LANES
    blocks = head_width // span
    fit = LANES // img_rows
    half = rows // 2
    chunks = rows // CHUNK
    scale = LANES ** (-0.5)
    f32, bf16 = jnp.float32, jnp.bfloat16
    right = (p, lax.rem(z + 1, n_seq))
    left = (p, lax.rem(z + n_seq - 1, n_seq))

    def lanes_of(n, size=LANES):
        return pl.ds(pl.multiple_of(n * size, size), size)

    def load(n, source, into):
        return pltpu.make_async_copy(source, into, load_sem.at[n])

    load_tiles, load_wk = load(0, tiles_hbm, tiles), load(1, wk_hbm, wk)
    load_wv, load_wd = load(2, wv_hbm, wv), load(3, wd_hbm, wd)
    load_up, load_gain = load(4, up_hbm, up), load(5, gain_hbm, gain)
    load_gate, load_lengths = load(6, gate_hbm, gate_s), load(7, length_hbm, lengths)
    load_reader, load_doc = load(8, reader_hbm, reader), load(9, doc_hbm, doc)
    load_query, load_grad = load(10, query_hbm, query), load(11, grad_hbm, grad)
    for copy in (load_tiles, load_wk, load_wd, load_up, load_gain, load_gate, load_lengths):
        copy.start()
    for copy in (load_reader, load_doc, load_wv):
        copy.start()
    barrier = pltpu.get_barrier_semaphore()
    loop(1, n_seq, lambda k: greet(barrier, (p, lax.rem(z + k, n_seq))))
    loop(1, n_dp, lambda k: greet(barrier, (lax.rem(p + k, n_dp), z)))

    def greet_back(k):
        @pl.when((k != 0) | (z != 0))
        def _():
            greet(barrier, (lax.rem(p + k, n_dp), k // fit))

    loop(0, n_dp, greet_back)

    def own_part(t, weight, own):
        ahead = lax.rem(z + 2 * n_seq - 1 - t, n_seq)
        back = lax.rem(z + 1 + t, n_seq)
        for side, head in ((0, ahead), (1, back)):
            part = pl.ds(side * half, half)
            own[part, :] = jnp.dot(
                tiles[part, :], weight[:, lanes_of(head)], preferred_element_type=f32
            )

    order = [c + side * (chunks // 2) for c in range(chunks // 2) for side in (0, 1)]

    def hop(sums, ss, rs, t, s):
        target = right if s < chunks // 2 else left
        part = pl.ds(s * CHUNK, CHUNK)
        return remote(sums.at[t, part], sums.at[t + 1, part], ss.at[t, s], rs.at[t, s], target)

    def k_hop(t, s):
        return hop(sum_k, k_ss, k_rs, t, s)

    def v_hop(t, s):
        return hop(sum_v, v_ss, v_rs, t, s)

    def k_step(t):
        own_part(t, wk, own_k)
        for s in order:
            part = pl.ds(s * CHUNK, CHUNK)
            k_hop(t - 1, s).wait_recv()
            sum_k[t, part, :] = sum_k[t, part, :] + own_k[part, :]
            k_hop(t, s).start()

    def v_step(t):
        own_part(t, wv, own_v)
        for s in order:
            part = pl.ds(s * CHUNK, CHUNK)
            v_hop(t - 1, s).wait_recv()
            sum_v[t, part, :] = (sum_v[t, part, :].astype(f32) + own_v[part, :]).astype(bf16)
            v_hop(t, s).start()

    load_tiles.wait()
    load_wk.wait()
    own_part(0, wk, own_k)
    sum_k[0] = own_k[...]
    pl.semaphore_wait(barrier, n_seq - 1 + n_dp - 1 + n_dp - jnp.where(z == 0, 1, 0))
    for s in order:
        k_hop(0, s).start()

    def low_copy(k):
        target = (p, lax.rem(z + k, n_seq))
        return remote(low_out, low_in.at[k], low_ss.at[k], low_rs.at[k], target)

    def up_copy(k, slot):
        target = (p, lax.rem(z + k, n_seq))
        return remote(up, up_all.at[slot], up_ss.at[k], up_rs.at[k], target)

    load_wd.wait()
    load_up.wait()
    low_own[...] = lax.dot_general(wd[...], tiles[...], NT, preferred_element_type=f32)
    low_out[...] = low_own[...].astype(bf16)
    loop(1, n_seq, lambda k: low_copy(k).start())
    loop(1, n_seq, lambda k: up_copy(k, z).start())
    up_all[z] = up[...]
    load_query.start()
    load_grad.start()
    for copy in (load_gain, load_gate, load_lengths, load_reader, load_doc):
        copy.wait()

    def find(g):
        at, mark = jnp.int32(0), jnp.int32(docs)
        for i in range(img_dev):
            hit = reader[i] == g
            at = jnp.where(hit, i, at)
            mark = jnp.where(hit, doc[i], mark)
        pick[g] = at
        tag[g] = mark

    loop(0, n_dp, find)

    def route(n, out, into, k):
        g = lax.rem(p + k, n_dp)
        return remote(
            out.at[k],
            into.at[pl.ds(pl.multiple_of(k * img_rows, img_rows), img_rows)],
            route_ss.at[n, k],
            route_rs.at[n, k],
            (g, z),
        )

    def k_route(k):
        return route(0, k_out, k_all.at[0], k)

    def v_route(k):
        return route(1, v_out, v_all.at[0], k)

    def ext_route(k):
        return route(2, ext_out, ext, k)

    lane = lax.broadcasted_iota(jnp.int32, (img_rows, LANES), 1)

    def ext_block(g):
        mark = jnp.where(lane == rank + tag[g], 1.0, 0.0)
        low = ext_rows[pick[g]].astype(f32)
        return jnp.where(lane < rank, low, mark).astype(bf16)

    def send_ext(k):
        ext_out[k] = ext_block(lax.rem(p + k, n_dp))
        ext_route(k).start()

    def low_finish():
        loop(1, n_seq, lambda k: low_copy(k).wait_send())
        low_total = low_own[...]
        for k in range(1, n_seq):
            low_copy(k).wait_recv()
            low_total = low_total + low_in[k].astype(f32)
        low_rank = low_total.astype(bf16)
        low_out[...] = low_rank
        eye = lax.broadcasted_iota(jnp.int32, (rank, LANES), 0) == lax.broadcasted_iota(
            jnp.int32, (rank, LANES), 1
        )
        eye = jnp.where(eye, 1.0, 0.0).astype(bf16)
        low_rows = lax.dot_general(low_rank, eye, TN, preferred_element_type=f32)
        ext_rows[...] = low_rows.astype(bf16).reshape(img_dev, img_rows, LANES)

    lag = min(LAG, n_seq - 2)
    if lag > 0:
        loop(1, lag, k_step)
        k_step(lag)
    load_wv.wait()
    own_part(0, wv, own_v)
    sum_v[0] = own_v[...].astype(bf16)
    for s in order:
        v_hop(0, s).start()
    low_finish()
    both_steps = n_seq - 2 - lag
    each = -(-(n_dp - 1) // max(1, both_steps))

    def both_step(t):
        first = 1 + (t - lag - 1) * each
        loop(first, jnp.minimum(first + each, n_dp), send_ext)
        k_step(t)
        v_step(t - lag)

    loop(lag + 1, n_seq - 1, both_step)
    if both_steps == 0:
        loop(1, n_dp, send_ext)

    per_chunk = CHUNK // img_rows
    own_part(n_seq - 1, wk, own_k)
    for s in order:
        part = pl.ds(s * CHUNK, CHUNK)
        k_hop(n_seq - 2, s).wait_recv()
        key_raw = sum_k[n_seq - 1, part, :] + own_k[part, :]
        mean_square = jnp.mean(key_raw * key_raw, axis=-1, keepdims=True)
        key_rows = (key_raw * lax.rsqrt(mean_square + EPS) * gain[...]).astype(bf16)
        rows_k[pl.ds(s * per_chunk, per_chunk)] = key_rows.reshape(per_chunk, img_rows, LANES)

    def send_k(k):
        k_out[k] = rows_k[pick[lax.rem(p + k, n_dp)]]
        k_route(k).start()

    loop(1, n_dp, send_k)
    k_all[0, :img_rows, :] = rows_k[pick[p]]
    ext[:img_rows, :] = ext_block(p)

    loop(n_seq - 1 - lag, n_seq - 1, v_step)
    own_part(n_seq - 1, wv, own_v)
    low_up = lax.dot_general(low_out[...], up[...], TN, preferred_element_type=f32)
    own_v[...] = own_v[...] + ADAPTER_SCALE * low_up
    for s in order:
        part = pl.ds(s * CHUNK, CHUNK)
        v_hop(n_seq - 2, s).wait_recv()
        value = (sum_v[n_seq - 1, part, :].astype(f32) + own_v[part, :]).astype(bf16)
        rows_v[pl.ds(s * per_chunk, per_chunk)] = value.reshape(per_chunk, img_rows, LANES)

    last = n_seq // 2 - 1
    part_rows = keys // PARTS
    slots = n_dp // PARTS

    def gather(held, n):
        def ahead(t, b):
            part = pl.ds(pl.multiple_of(b * part_rows, part_rows), part_rows)
            source, into = lax.rem(n_seq - t, n_seq), n_seq - 1 - t
            return remote(
                held.at[source, part],
                held.at[into, part],
                ring_ss.at[n, t, b],
                ring_rs.at[n, t, b],
                right,
            )

        def back(t, b):
            part = pl.ds(pl.multiple_of(b * part_rows, part_rows), part_rows)
            return remote(
                held.at[t, part],
                held.at[t + 1, part],
                ring_ss.at[n + 1, t, b],
                ring_rs.at[n + 1, t, b],
                left,
            )

        return ((ahead, lambda b: b < PARTS // 2), (back, lambda b: b >= PARTS // 2))

    k_ways, v_ways = gather(k_all, 0), gather(v_all, 2)

    def gather_start(ways, arrived):
        for b in range(PARTS):
            loop(max(1, b * slots), (b + 1) * slots, lambda k: arrived(k).wait_recv())
            for way, whole in ways:
                if last > 0 or whole(b):
                    way(0, b).start()

    def forward(ways, t, b):
        for way, whole in ways:

            @pl.when((t <= last) | whole(b))
            def _():
                way(t - 1, b).wait_recv()

            @pl.when((t < last) | ((t == last) & whole(b)))
            def _():
                way(t, b).start()

    def after_block(ways, m):
        i = m // blocks
        step = (i + 1) // 2
        q = m - blocks * (2 * step - 1)
        per = PARTS // (2 * blocks)

        @pl.when(m == blocks - 1)
        def _():
            loop(0, PARTS, lambda b: forward(ways, 1, b))

        @pl.when((i >= 1) & (i < n_seq - 1))
        def _():
            loop(q * per, (q + 1) * per, lambda b: forward(ways, step + 1, b))

    def gather_sent(ways):
        for t in range(last + 1):
            for b in range(PARTS):
                for way, whole in ways:
                    if t < last or whole(b):
                        way(t, b).wait_send()

    gather_start(k_ways, k_route)

    def send_v(k):
        v_out[k] = rows_v[pick[lax.rem(p + k, n_dp)]]
        v_route(k).start()

    loop(1, n_dp, send_v)
    v_all[0, :img_rows, :] = rows_v[pick[p]]

    lane_tok = lax.broadcasted_iota(jnp.int32, (tokens, LANES), 1)
    place = lax.broadcasted_iota(jnp.int32, (tokens, LANES), 0) + z * tokens
    own_doc = jnp.zeros((tokens, LANES), jnp.int32)
    end = jnp.int32(0)
    for d in range(docs - 1):
        end = end + lengths[0, d]
        own_doc = own_doc + jnp.where(place >= end, 1, 0)
    other = (lane_tok >= rank) & (lane_tok <= rank + docs) & (lane_tok != rank + own_doc)
    penalty = jnp.where(other, MASKED, 0.0).astype(bf16)
    for n in range(block // tokens):
        bias[n * tokens : (n + 1) * tokens, :] = penalty
    small[...] = jnp.zeros_like(small)
    gate = jnp.tanh(jnp.full((1, LANES), gate_s[0], f32))
    loop(1, n_seq, lambda k: up_copy(k, lax.rem(z + n_seq - k, n_seq)).wait_recv())
    loop(1, n_dp, lambda k: ext_route(k).wait_recv())
    ext_t[...] = ext[...].T
    load_query.wait()
    load_grad.wait()

    def stack(ref, cols):
        part = ref[:, cols]
        return jnp.concatenate(
            [part[:, n * LANES : (n + 1) * LANES] for n in range(block // tokens)], axis=0
        )

    def unstack(x):
        return jnp.concatenate(
            [x[n * tokens : (n + 1) * tokens] for n in range(block // tokens)], axis=1
        )

    def where_is(m):
        i, j = m // blocks, lax.rem(m, blocks)
        slot = jnp.where(lax.rem(i, 2) == 1, n_seq - (i + 1) // 2, i // 2)
        head = lax.rem(z + slot, n_seq)
        cols = pl.ds(pl.multiple_of(head * head_width + j * span, span), span)
        return i, j, slot, head, cols

    def first_half(m):
        i, j, slot, head, cols = where_is(m)
        g = (gate * stack(grad, cols).astype(f32)).astype(bf16)
        grad[:, cols] = unstack(g)
        q = jnp.concatenate([stack(query, cols), bias[...]], axis=1)
        key_ext = jnp.concatenate([k_all[slot], ext[...]], axis=1)
        scores = lax.dot_general(q, key_ext, NT, preferred_element_type=f32)
        row_max = jnp.max(scores, axis=1, keepdims=True)
        weights = jnp.exp2((scores - row_max) * (scale * LOG2_E))
        prob = weights * (1.0 / jnp.sum(weights, axis=1, keepdims=True))
        prob = prob.astype(bf16)
        probs[i, pl.ds(pl.multiple_of(j * block, block), block), :] = prob
        part = lax.dot_general(g, prob, TN, preferred_element_type=f32)

        @pl.when(j == 0)
        def _():
            value_grad[...] = part

        @pl.when(j > 0)
        def _():
            value_grad[...] += part

        @pl.when(j == blocks - 1)
        def _():
            whole = value_grad[...].astype(bf16)
            small[:rank, :] += jnp.dot(up_all[head], whole, preferred_element_type=f32)
            small[rank:, lanes_of(head)] = lax.dot_general(
                ext_t[:rank, :], whole, NT, preferred_element_type=f32
            )

        @pl.when(m == max(blocks * (2 * last - 1), blocks) - 1)
        def _():
            gather_start(v_ways, v_route)

        after_block(k_ways, m)

    loop(0, n_seq * blocks, first_half)

    def col_copy(k):
        target = lax.rem(z + k, n_seq)
        return remote(
            small.at[:, lanes_of(target)], col_in.at[k], col_ss.at[k], col_rs.at[k], (p, target)
        )

    wide = total.shape[1]
    pieces = 2 * (wide // LANES)

    def back_copy(n):
        j, s = lax.rem(n, fit), n // fit
        o = lax.rem(p + n_dp - fit * z - j, n_dp)
        return remote(back_out.at[j], back_in.at[p], back_ss.at[n], back_rs.at[p], (o, s))

    def unless_own(n, act):
        pl.when((n != 0) | (z != 0))(act)

    def piece_of(j):
        return total.at[
            pl.ds(pl.multiple_of(lax.rem(j, 2) * 8, 8), 8),
            lanes_of(j // 2),
        ]

    def sum_copy(j):
        k = lax.rem(j - p + n_dp, n_dp)
        return remote(piece_of(j), sum_in.at[k], sum_ss.at[j], sum_rs.at[k], (j, z))

    def done_copy(k, j):
        g = lax.rem(p + k, n_dp)
        return remote(done.at[j], done.at[j], done_ss.at[k], done_rs.at[j], (g, z))

    def adapter_back():
        own = small[:, lanes_of(z)]
        for k in range(1, n_seq):
            col_copy(k).wait_recv()
            own = own + col_in[k]
        own = ADAPTER_SCALE * own
        for j in range(fit):
            moved = own[:rank]
            if j > 0:
                moved = pltpu.roll(moved, LANES - j * img_rows, 1)
            back_out[j] = moved.astype(bf16)
        total[:, width:] = jnp.zeros((rank, wide - width), f32)
        total[:, wide - LANES :] = own[rank:]
        loop(0, fit * n_seq, lambda n: unless_own(n, lambda: back_copy(n).start()))

        @pl.when(z == 0)
        def _():
            back_in[p] = back_out[0]

    def adapter_sum():
        def back_wait(k):
            g = lax.rem(p + k, n_dp)
            copy = remote(
                back_out.at[0], back_in.at[g], back_ss.at[0], back_rs.at[g], (g, k // fit)
            )
            unless_own(k, lambda: copy.wait_recv())

        loop(0, n_dp, back_wait)
        lane_rank = lax.broadcasted_iota(jnp.int32, (rank, LANES), 1)
        pieces_in = []
        for first in range(0, img_dev, fit):
            piece = jnp.zeros((rank, LANES), f32)
            for i in range(fit):
                held = back_in[reader[first + i]].astype(f32)
                if i > 0:
                    held = pltpu.roll(held, i * img_rows, 1)
                piece = jnp.where(lane_rank // img_rows == i, held, piece)
            pieces_in.append(piece.astype(bf16))
        total[:, :width] = jnp.dot(
            jnp.concatenate(pieces_in, axis=1), tiles[...], preferred_element_type=f32
        )
        loop(0, pieces, lambda j: pl.when(j != p)(lambda: sum_copy(j).start()))

    def adapter_done():
        @pl.when(p < pieces)
        def _():
            def take(k, acc):
                remote(
                    piece_of(p), sum_in.at[k], sum_ss.at[0], sum_rs.at[k], (p, z)
                ).wait_recv()
                return acc + sum_in[k]

            done[p] = lax.fori_loop(1, n_dp, take, piece_of(p)[...])
            loop(1, n_dp, lambda k: done_copy(k, p).start())

    loop(1, n_seq, lambda k: col_copy(k).start())

    def store(n, i, head):
        cols = lanes_of(head, head_width)
        source, into = ((gated, gated_hbm), (query_grad, query_grad_hbm))[n]
        return pltpu.make_async_copy(source.at[:, cols], into.at[:, cols], store_sem.at[n, i])

    end_block = n_seq * blocks - 1

    def second_half(m):
        i, j, slot, head, cols = where_is(m)
        g = stack(grad, cols)
        prob = probs[i, pl.ds(pl.multiple_of(j * block, block), block), :]
        value = v_all[slot]
        attended = jnp.dot(prob, value, preferred_element_type=f32)
        prob_grad = lax.dot_general(g, value, NT, preferred_element_type=f32)
        gated[:, cols] = unstack((gate * attended).astype(bf16))
        delta = jnp.sum(g.astype(f32) * attended, axis=1, keepdims=True)
        score_grad = (prob.astype(f32) * (prob_grad - delta)).astype(bf16)
        out_grad = jnp.dot(score_grad, k_all[slot], preferred_element_type=f32)
        query_grad[:, cols] = unstack((out_grad * scale).astype(bf16))

        @pl.when(j == blocks - 1)
        def _():
            store(0, i, head).start()
            store(1, i, head).start()

        after_block(v_ways, m)
        pl.when(m == blocks - 1)(adapter_back)
        pl.when(m == min(3 * blocks - 1, end_block))(adapter_sum)
        pl.when(m == min(5 * blocks - 1, end_block))(adapter_done)

    loop(0, n_seq * blocks, second_half)

    loop(0, pieces, lambda j: pl.when(j != p)(lambda: done_copy(0, j).wait_recv()))
    for j in range(pieces - 2):
        r, c = 8 * (j % 2), LANES * (j // 2)
        fill = min(LANES, width - c)
        if fill > 0:
            down_stage[r : r + 8, c : c + fill] = done[j][:, :fill]
    up_stage[:8, :] = done[pieces - 2]
    up_stage[8:, :] = done[pieces - 1]
    store_down = pltpu.make_async_copy(down_stage, down_hbm, out_sem.at[0])
    store_up = pltpu.make_async_copy(up_stage, up_out_hbm, out_sem.at[1])
    store_down.start()
    store_up.start()

    def ring_sent(t):
        for s in range(chunks):
            k_hop(t, s).wait_send()
            v_hop(t, s).wait_send()

    loop(0, n_seq - 1, ring_sent)
    loop(1, n_seq, lambda k: up_copy(k, z).wait_send())
    for routed in (k_route, v_route, ext_route):
        loop(1, n_dp, lambda k: routed(k).wait_send())
    gather_sent(k_ways)
    gather_sent(v_ways)
    loop(1, n_seq, lambda k: col_copy(k).wait_send())
    loop(0, fit * n_seq, lambda n: unless_own(n, lambda: back_copy(n).wait_send()))
    loop(0, pieces, lambda j: pl.when(j != p)(lambda: sum_copy(j).wait_send()))

    @pl.when(p < pieces)
    def _():
        loop(1, n_dp, lambda k: done_copy(k, p).wait_send())

    def stored(m):
        i, j, slot, head, cols = where_is(m * blocks)
        store(0, i, head).wait()
        store(1, i, head).wait()

    loop(0, n_seq, stored)
    store_down.wait()
    store_up.wait()


def per_device(
    queries,
    output_gradient,
    tiles,
    frozen_key_weight,
    frozen_value_weight,
    key_norm_gain,
    adapter_down_weight,
    adapter_up_weight,
    gate,
    document_lengths,
    image_reader_group,
    image_document,
):
    n_dp, n_seq = lax.axis_size("dp"), lax.axis_size("seq")
    docs = document_lengths.shape[1]
    rank = adapter_up_weight.shape[0]
    img_dev, img_rows, width = tiles.shape
    rows = img_dev * img_rows
    tokens, columns = queries.shape
    keys = n_dp * img_rows
    block = min(HEADS_AT_ONCE * LANES, columns // n_seq) // LANES * tokens
    wide = -(-width // LANES) * LANES + LANES
    pieces = 2 * (wide // LANES)
    fit = LANES // img_rows
    fan = fit * n_seq
    chunks = rows // CHUNK
    any_space = pl.BlockSpec(memory_space=pl.ANY)
    f32, bf16 = jnp.float32, jnp.bfloat16

    def held(*shape, kind=bf16):
        return pltpu.VMEM(shape, kind)

    dma = pltpu.SemaphoreType.DMA
    gated, query_grad, down_rows, up_grad = pl.pallas_call(
        functools.partial(fused_kernel, n_dp, n_seq, docs),
        out_shape=(
            jax.ShapeDtypeStruct((tokens, columns), bf16),
            jax.ShapeDtypeStruct((tokens, columns), bf16),
            jax.ShapeDtypeStruct((rank, width), f32),
            jax.ShapeDtypeStruct((rank, LANES), f32),
        ),
        in_specs=[any_space] * 12,
        out_specs=(any_space,) * 4,
        scratch_shapes=[
            held(tokens, columns),
            held(tokens, columns),
            held(tokens, columns),
            held(tokens, columns),
            held(rows, width),
            held(width, n_seq * LANES),
            held(width, n_seq * LANES),
            held(rank, width),
            held(rank, LANES),
            held(1, LANES, kind=f32),
            pltpu.SMEM((1,), f32),
            pltpu.SMEM((1, docs), jnp.int32),
            pltpu.SMEM((img_dev,), jnp.int32),
            pltpu.SMEM((img_dev,), jnp.int32),
            held(rows, LANES, kind=f32),
            held(rows, LANES, kind=f32),
            held(n_seq, rows, LANES, kind=f32),
            held(n_seq, rows, LANES),
            held(rank, rows, kind=f32),
            held(rank, rows),
            held(n_seq, rank, rows),
            held(n_seq, rank, LANES),
            pltpu.SMEM((n_dp,), jnp.int32),
            pltpu.SMEM((n_dp,), jnp.int32),
            held(img_dev, img_rows, LANES),
            held(img_dev, img_rows, LANES),
            held(img_dev, img_rows, LANES),
            held(n_dp, img_rows, LANES),
            held(n_dp, img_rows, LANES),
            held(n_dp, img_rows, LANES),
            held(n_seq, keys, LANES),
            held(n_seq, keys, LANES),
            held(keys, LANES),
            held(LANES, keys),
            held(block, LANES),
            held(n_seq, columns // n_seq // LANES * tokens, keys),
            held(LANES, keys, kind=f32),
            held(2 * rank, keys, kind=f32),
            held(n_seq, 2 * rank, LANES, kind=f32),
            held(fit, rank, LANES),
            held(n_dp, rank, LANES),
            held(rank, wide, kind=f32),
            held(n_dp, 8, LANES, kind=f32),
            held(pieces, 8, LANES, kind=f32),
            held(rank, width, kind=f32),
            held(rank, LANES, kind=f32),
            dma((12,)),
            dma((2, n_seq)),
            dma((2,)),
            dma((n_seq, chunks)),
            dma((n_seq, chunks)),
            dma((n_seq, chunks)),
            dma((n_seq, chunks)),
            dma((n_seq,)),
            dma((n_seq,)),
            dma((n_seq,)),
            dma((n_seq,)),
            dma((3, n_dp)),
            dma((3, n_dp)),
            dma((4, n_seq // 2, PARTS)),
            dma((4, n_seq // 2, PARTS)),
            dma((n_seq,)),
            dma((n_seq,)),
            dma((fan,)),
            dma((n_dp,)),
            dma((pieces,)),
            dma((n_dp,)),
            dma((n_dp,)),
            dma((pieces,)),
        ],
        compiler_params=pltpu.CompilerParams(
            collective_id=0, has_side_effects=True, vmem_limit_bytes=58 << 20
        ),
    )(
        queries,
        output_gradient,
        tiles.reshape(rows, width),
        frozen_key_weight,
        frozen_value_weight,
        adapter_down_weight.T,
        adapter_up_weight,
        key_norm_gain.reshape(1, -1),
        gate,
        document_lengths,
        image_reader_group,
        image_document,
    )
    return (gated, query_grad, down_rows.T, up_grad)


def solution(mesh):
    placed = (
        P(("dp", "seq"), None),
        P(("dp", "seq"), None),
        P("dp", None, "seq"),
        P("seq", None),
        P("seq", None),
        P(),
        P("seq", None),
        P(None, "seq"),
        P(),
        P("dp", None),
        P("dp"),
        P("dp"),
    )
    return jax.shard_map(
        per_device,
        mesh=mesh,
        in_specs=placed,
        out_specs=(P(("dp", "seq"), None), P(("dp", "seq"), None), P("seq", None), P(None, "seq")),
        check_vma=False,
    )
```

```python
import functools

import jax
import jax.numpy as jnp
from jax import lax
from jax.experimental import pallas as pl
from jax.experimental.pallas import tpu as pltpu
from jax.sharding import PartitionSpec as P

EPS = 1e-05
ADAPTER_SCALE = 2.0
MASKED = -1e30
LANES = 128
PARTS = 4
HEADS_AT_ONCE = 4
LOG2_E = 1.4426950408889634
MESH = pl.DeviceIdType.MESH
NT = (((1,), (1,)), ((), ()))
TN = (((0,), (0,)), ((), ()))


def remote(src, dst, send_sem, recv_sem, target):
    return pltpu.make_async_remote_copy(
        src_ref=src,
        dst_ref=dst,
        send_sem=send_sem,
        recv_sem=recv_sem,
        device_id=target,
        device_id_type=MESH,
    )


def loop(first, last, body):
    def step(i, carry):
        body(i)
        return carry

    lax.fori_loop(first, last, step, 0)


def greet(barrier, target):
    pl.semaphore_signal(barrier, inc=1, device_id=target, device_id_type=MESH)


def fused_kernel(
    n_dp,
    n_seq,
    docs,
    query_hbm,
    grad_hbm,
    tiles_hbm,
    wk_hbm,
    wv_hbm,
    wd_hbm,
    up_hbm,
    gain_hbm,
    gate_hbm,
    length_hbm,
    reader_hbm,
    doc_hbm,
    gated_hbm,
    query_grad_hbm,
    down_hbm,
    up_out_hbm,
    query,
    grad,
    gated,
    query_grad,
    tiles,
    wk,
    wv,
    wd,
    up,
    gain,
    gate_s,
    lengths,
    reader,
    doc,
    own,
    sum_k,
    sum_v,
    low_own,
    low_out,
    low_in,
    up_all,
    pick,
    tag,
    rows_k,
    rows_v,
    ext_rows,
    k_out,
    v_out,
    ext_out,
    k_all,
    v_all,
    ext,
    ext_t,
    bias,
    probs,
    value_grad,
    small,
    col_in,
    back_out,
    back_in,
    total,
    sum_in,
    done,
    down_stage,
    up_stage,
    load_sem,
    store_sem,
    sent_sem,
    all_sem,
    sum_sem,
    route_sem,
    ring_sem,
    done_sem,
):
    p = lax.axis_index("dp")
    z = lax.axis_index("seq")
    rows, width = tiles.shape
    tokens, columns = query.shape
    rank = up.shape[0]
    img_dev, img_rows = rows_k.shape[:2]
    keys = ext.shape[0]
    head_width = columns // n_seq
    block = bias.shape[0]
    span = (block // tokens) * LANES
    blocks = head_width // span
    fit = LANES // img_rows
    half = rows // 2
    mid = n_seq // 2
    sum_rows = rows // PARTS
    scale = LANES ** (-0.5)
    f32, bf16 = jnp.float32, jnp.bfloat16
    right = (p, lax.rem(z + 1, n_seq))
    left = (p, lax.rem(z + n_seq - 1, n_seq))

    def lanes_of(n, size=LANES):
        return pl.ds(pl.multiple_of(n * size, size), size)

    def load(n, source, into):
        return pltpu.make_async_copy(source, into, load_sem.at[n])

    load_tiles, load_wk = load(0, tiles_hbm, tiles), load(1, wk_hbm, wk)
    load_wv, load_wd = load(2, wv_hbm, wv), load(3, wd_hbm, wd)
    load_up, load_gain = load(4, up_hbm, up), load(5, gain_hbm, gain)
    load_gate, load_lengths = load(6, gate_hbm, gate_s), load(7, length_hbm, lengths)
    load_reader, load_doc = load(8, reader_hbm, reader), load(9, doc_hbm, doc)
    load_query, load_grad = load(10, query_hbm, query), load(11, grad_hbm, grad)
    for copy in (load_tiles, load_wk, load_wd, load_up, load_gain, load_gate, load_lengths):
        copy.start()
    for copy in (load_reader, load_doc, load_wv):
        copy.start()
    barrier = pltpu.get_barrier_semaphore()
    loop(1, n_seq, lambda k: greet(barrier, (p, lax.rem(z + k, n_seq))))
    loop(1, n_dp, lambda k: greet(barrier, (lax.rem(p + k, n_dp), z)))

    def greet_back(k):
        @pl.when((k != 0) | (z != 0))
        def _():
            greet(barrier, (lax.rem(p + k, n_dp), k // fit))

    loop(0, n_dp, greet_back)

    def all_sent(n, region):
        remote(region, region, sent_sem.at[n], all_sem.at[0], right).wait_send()

    def all_here(region, sem):
        remote(region, region, sent_sem.at[0], sem, right).wait_recv()

    def in_part(b):
        return pl.ds(b * sum_rows, sum_rows)

    def goes(side, b):
        return (b < PARTS // 2) == (side == 0)

    def hop(n, side, t, b):
        sums = (sum_k, sum_v)[n]
        at = side * (mid + 1) + t
        return remote(
            sums.at[at, in_part(b)],
            sums.at[at + 1, in_part(b)],
            sent_sem.at[n],
            sum_sem.at[n, side, t, b],
            (right, left)[side],
        )

    def own_part(n, head):
        weight = (wk, wv)[n]
        return jnp.dot(tiles[...], weight[:, lanes_of(head)], preferred_element_type=f32)

    def first_sums(n):
        sums = (sum_k, sum_v)[n]
        part = own_part(n, lax.rem(z + mid, n_seq)).astype(sums.dtype)
        sums[0, :half, :] = part[:half]
        sums[mid + 1, half:, :] = part[half:]

    def first_sends(n):
        for b in range(PARTS):
            hop(n, 0 if goes(0, b) else 1, 0, b).start()

    def sum_step(n, t):
        sums = (sum_k, sum_v)[n]
        own[0] = own_part(n, lax.rem(z + mid - t, n_seq))
        own[1] = own_part(n, lax.rem(z + mid + t, n_seq))
        for c in range(PARTS):
            for side in (0, 1):
                b = c if side == 0 else (c + PARTS // 2) % PARTS
                at = side * (mid + 1) + t
                total_here = own[side, in_part(b), :]
                if t > 1 or goes(side, b):
                    hop(n, side, t - 1, b).wait_recv()
                    total_here = total_here + sums[at, in_part(b), :].astype(f32)
                sums[at, in_part(b), :] = total_here.astype(sums.dtype)
                hop(n, side, t, b).start()

    def last_sums(n, b):
        sums = (sum_k, sum_v)[n]
        total_here = own[0, in_part(b), :]
        for side in (0, 1):
            if mid > 1 or goes(side, b):
                hop(n, side, mid - 1, b).wait_recv()
                at = side * (mid + 1) + mid
                total_here = total_here + sums[at, in_part(b), :].astype(f32)
        return total_here

    load_tiles.wait()
    load_wk.wait()
    first_sums(0)
    pl.semaphore_wait(barrier, n_seq - 1 + n_dp - 1 + n_dp - jnp.where(z == 0, 1, 0))
    first_sends(0)

    def low_copy(k):
        target = (p, lax.rem(z + k, n_seq))
        return remote(low_out, low_in.at[k], sent_sem.at[2], all_sem.at[1], target)

    def up_copy(k):
        target = (p, lax.rem(z + k, n_seq))
        return remote(up, up_all.at[k], sent_sem.at[3], all_sem.at[2], target)

    others = pl.ds(1, n_seq - 1)

    load_wd.wait()
    load_up.wait()
    low_own[...] = lax.dot_general(wd[...], tiles[...], NT, preferred_element_type=f32)
    low_out[...] = low_own[...].astype(bf16)
    loop(1, n_seq, lambda k: low_copy(k).start())
    loop(1, n_seq, lambda k: up_copy(k).start())
    up_all[0] = up[...]
    load_query.start()
    load_grad.start()
    for copy in (load_gain, load_gate, load_lengths, load_reader, load_doc):
        copy.wait()

    def find(g):
        at, mark = jnp.int32(0), jnp.int32(docs)
        for i in range(img_dev):
            hit = reader[i] == g
            at = jnp.where(hit, i, at)
            mark = jnp.where(hit, doc[i], mark)
        pick[g] = at
        tag[g] = mark

    loop(0, n_dp, find)

    part_rows = keys // PARTS
    slots = n_dp // PARTS

    def routed(n, into, b):
        skip = img_rows if b == 0 else 0
        part = into.at[pl.ds(b * part_rows + skip, part_rows - skip)]
        all_here(part, route_sem.at[n, b])

    def route(n, out, into, k):
        g = lax.rem(p + k, n_dp)
        return remote(
            out.at[k],
            into.at[pl.ds(pl.multiple_of(k * img_rows, img_rows), img_rows)],
            sent_sem.at[4 + n],
            route_sem.at[n, k // slots],
            (g, z),
        )

    def k_route(k):
        return route(0, k_out, k_all.at[0], k)

    def v_route(k):
        return route(1, v_out, v_all.at[0], k)

    def ext_route(k):
        return route(2, ext_out, ext, k)

    lane = lax.broadcasted_iota(jnp.int32, (img_rows, LANES), 1)

    def ext_block(g):
        mark = jnp.where(lane == rank + tag[g], 1.0, 0.0)
        low = ext_rows[pick[g]].astype(f32)
        return jnp.where(lane < rank, low, mark).astype(bf16)

    def send_ext(k):
        ext_out[k] = ext_block(lax.rem(p + k, n_dp))
        ext_route(k).start()

    def low_finish():
        all_sent(2, low_in.at[others])
        all_here(low_in.at[others], all_sem.at[1])
        low_total = low_own[...]
        for k in range(1, n_seq):
            low_total = low_total + low_in[k].astype(f32)
        low_rank = low_total.astype(bf16)
        low_out[...] = low_rank
        eye = lax.broadcasted_iota(jnp.int32, (rank, LANES), 0) == lax.broadcasted_iota(
            jnp.int32, (rank, LANES), 1
        )
        eye = jnp.where(eye, 1.0, 0.0).astype(bf16)
        low_rows = lax.dot_general(low_rank, eye, TN, preferred_element_type=f32)
        ext_rows[...] = low_rows.astype(bf16).reshape(img_dev, img_rows, LANES)

    for t in range(1, mid):
        if t == mid - 1:
            low_finish()
            loop(1, n_dp, send_ext)
        sum_step(0, t)
    if mid == 1:
        low_finish()
        loop(1, n_dp, send_ext)
    load_wv.wait()
    first_sums(1)
    first_sends(1)

    per_part = sum_rows // img_rows
    own[0] = own_part(0, z)
    for b in range(PARTS):
        key_raw = last_sums(0, b)
        mean_square = jnp.mean(key_raw * key_raw, axis=-1, keepdims=True)
        key_rows = (key_raw * lax.rsqrt(mean_square + EPS) * gain[...]).astype(bf16)
        rows_k[pl.ds(b * per_part, per_part)] = key_rows.reshape(per_part, img_rows, LANES)

    def send_k(k):
        k_out[k] = rows_k[pick[lax.rem(p + k, n_dp)]]
        k_route(k).start()

    loop(1, n_dp, send_k)
    k_all[0, :img_rows, :] = rows_k[pick[p]]
    ext[:img_rows, :] = ext_block(p)

    for t in range(1, mid):
        sum_step(1, t)
    low_up = lax.dot_general(low_out[...], up[...], TN, preferred_element_type=f32)
    own[0] = own_part(1, z) + ADAPTER_SCALE * low_up
    for b in range(PARTS):
        value = last_sums(1, b).astype(bf16)
        rows_v[pl.ds(b * per_part, per_part)] = value.reshape(per_part, img_rows, LANES)

    last = mid - 1

    def gather(held, n):
        def ahead(t, b):
            part = pl.ds(pl.multiple_of(b * part_rows, part_rows), part_rows)
            source, into = lax.rem(n_seq - t, n_seq), n_seq - 1 - t
            return remote(
                held.at[source, part],
                held.at[into, part],
                sent_sem.at[7 + n // 2],
                ring_sem.at[n, t, b],
                right,
            )

        def back(t, b):
            part = pl.ds(pl.multiple_of(b * part_rows, part_rows), part_rows)
            return remote(
                held.at[t, part],
                held.at[t + 1, part],
                sent_sem.at[7 + n // 2],
                ring_sem.at[n + 1, t, b],
                left,
            )

        return ((ahead, lambda b: b < PARTS // 2), (back, lambda b: b >= PARTS // 2))

    k_ways, v_ways = gather(k_all, 0), gather(v_all, 2)

    def gather_start(ways, n, held):
        for b in range(PARTS):
            routed(n, held.at[0], b)
            for way, whole in ways:
                if last > 0 or whole(b):
                    way(0, b).start()

    def forward(ways, t, b):
        for way, whole in ways:

            @pl.when((t <= last) | whole(b))
            def _():
                way(t - 1, b).wait_recv()

            @pl.when((t < last) | ((t == last) & whole(b)))
            def _():
                way(t, b).start()

    def after_block(ways, m):
        i = m // blocks
        step = (i + 1) // 2
        q = m - blocks * (2 * step - 1)
        per = PARTS // (2 * blocks)

        @pl.when(m == blocks - 1)
        def _():
            loop(0, PARTS, lambda b: forward(ways, 1, b))

        @pl.when((i >= 1) & (i < n_seq - 1))
        def _():
            loop(q * per, (q + 1) * per, lambda b: forward(ways, step + 1, b))

    gather_start(k_ways, 0, k_all)

    def send_v(k):
        v_out[k] = rows_v[pick[lax.rem(p + k, n_dp)]]
        v_route(k).start()

    loop(1, n_dp, send_v)
    v_all[0, :img_rows, :] = rows_v[pick[p]]

    lane_tok = lax.broadcasted_iota(jnp.int32, (tokens, LANES), 1)
    place = lax.broadcasted_iota(jnp.int32, (tokens, LANES), 0) + z * tokens
    own_doc = jnp.zeros((tokens, LANES), jnp.int32)
    end = jnp.int32(0)
    for d in range(docs - 1):
        end = end + lengths[0, d]
        own_doc = own_doc + jnp.where(place >= end, 1, 0)
    other = (lane_tok >= rank) & (lane_tok <= rank + docs) & (lane_tok != rank + own_doc)
    penalty = jnp.where(other, MASKED, 0.0).astype(bf16)
    for n in range(block // tokens):
        bias[n * tokens : (n + 1) * tokens, :] = penalty
    small[...] = jnp.zeros_like(small)
    gate = jnp.tanh(jnp.full((1, LANES), gate_s[0], f32))
    all_here(up_all.at[others], all_sem.at[2])
    for b in range(PARTS):
        routed(2, ext, b)
    ext_t[...] = ext[...].T
    load_query.wait()
    load_grad.wait()

    def stack(ref, cols):
        part = ref[:, cols]
        return jnp.concatenate(
            [part[:, n * LANES : (n + 1) * LANES] for n in range(block // tokens)], axis=0
        )

    def unstack(x):
        return jnp.concatenate(
            [x[n * tokens : (n + 1) * tokens] for n in range(block // tokens)], axis=1
        )

    def where_is(m):
        i, j = m // blocks, lax.rem(m, blocks)
        slot = jnp.where(lax.rem(i, 2) == 1, n_seq - (i + 1) // 2, i // 2)
        head = lax.rem(z + slot, n_seq)
        cols = pl.ds(pl.multiple_of(head * head_width + j * span, span), span)
        return i, j, slot, head, cols

    def first_half(m):
        i, j, slot, head, cols = where_is(m)
        g = (gate * stack(grad, cols).astype(f32)).astype(bf16)
        grad[:, cols] = unstack(g)
        q = jnp.concatenate([stack(query, cols), bias[...]], axis=1)
        key_ext = jnp.concatenate([k_all[slot], ext[...]], axis=1)
        scores = lax.dot_general(q, key_ext, NT, preferred_element_type=f32)
        row_max = jnp.max(scores, axis=1, keepdims=True)
        weights = jnp.exp2((scores - row_max) * (scale * LOG2_E))
        prob = weights * (1.0 / jnp.sum(weights, axis=1, keepdims=True))
        prob = prob.astype(bf16)
        probs[i, pl.ds(pl.multiple_of(j * block, block), block), :] = prob
        part = lax.dot_general(g, prob, TN, preferred_element_type=f32)

        @pl.when(j == 0)
        def _():
            value_grad[...] = part

        @pl.when(j > 0)
        def _():
            value_grad[...] += part

        @pl.when(j == blocks - 1)
        def _():
            whole = value_grad[...].astype(bf16)
            small[:rank, :] += jnp.dot(
                up_all[lax.rem(n_seq - slot, n_seq)], whole, preferred_element_type=f32
            )
            small[rank:, lanes_of(head)] = lax.dot_general(
                ext_t[:rank, :], whole, NT, preferred_element_type=f32
            )

        @pl.when(m == max(blocks * (2 * last - 1), blocks) - 1)
        def _():
            gather_start(v_ways, 1, v_all)

        after_block(k_ways, m)

    loop(0, n_seq * blocks, first_half)

    def col_copy(k):
        target = lax.rem(z + k, n_seq)
        return remote(
            small.at[:, lanes_of(target)], col_in.at[k], sent_sem.at[9], all_sem.at[3], (p, target)
        )

    wide = total.shape[1]
    pieces = 2 * (wide // LANES)

    def back_copy(n):
        j, s = lax.rem(n, fit), n // fit
        o = lax.rem(p + n_dp - fit * z - j, n_dp)
        into = back_in.at[fit * z + j]
        return remote(back_out.at[j], into, sent_sem.at[10], all_sem.at[4], (o, s))

    def unless_own(n, act):
        pl.when((n != 0) | (z != 0))(act)

    def piece_of(j):
        return total.at[
            pl.ds(pl.multiple_of(lax.rem(j, 2) * 8, 8), 8),
            lanes_of(j // 2),
        ]

    def sum_copy(j):
        k = lax.rem(j - p + n_dp, n_dp)
        return remote(piece_of(j), sum_in.at[k], sent_sem.at[11], all_sem.at[0], (j, z))

    def done_copy(k, j):
        g = lax.rem(p + k, n_dp)
        return remote(done.at[j], done.at[j], sent_sem.at[12], done_sem.at[j], (g, z))

    def adapter_back():
        mine = small[:, lanes_of(z)]
        all_here(col_in.at[others], all_sem.at[3])
        for k in range(1, n_seq):
            mine = mine + col_in[k]
        mine = ADAPTER_SCALE * mine
        for j in range(fit):
            moved = mine[:rank]
            if j > 0:
                moved = pltpu.roll(moved, LANES - j * img_rows, 1)
            back_out[j] = moved.astype(bf16)
        total[:, width:] = jnp.zeros((rank, wide - width), f32)
        total[:, wide - LANES :] = mine[rank:]
        loop(0, fit * n_seq, lambda n: unless_own(n, lambda: back_copy(n).start()))

        @pl.when(z == 0)
        def _():
            back_in[0] = back_out[0]

    def adapter_sum():
        @pl.when(z == 0)
        def _():
            all_here(back_in.at[pl.ds(1, n_dp - 1)], all_sem.at[4])

        @pl.when(z != 0)
        def _():
            all_here(back_in, all_sem.at[4])

        lane_rank = lax.broadcasted_iota(jnp.int32, (rank, LANES), 1)
        pieces_in = []
        for first in range(0, img_dev, fit):
            piece = jnp.zeros((rank, LANES), f32)
            for i in range(fit):
                held = back_in[lax.rem(reader[first + i] - p + n_dp, n_dp)].astype(f32)
                if i > 0:
                    held = pltpu.roll(held, i * img_rows, 1)
                piece = jnp.where(lane_rank // img_rows == i, held, piece)
            pieces_in.append(piece.astype(bf16))
        total[:, :width] = jnp.dot(
            jnp.concatenate(pieces_in, axis=1), tiles[...], preferred_element_type=f32
        )
        loop(0, pieces, lambda j: pl.when(j != p)(lambda: sum_copy(j).start()))

    def adapter_done():
        @pl.when(p < pieces)
        def _():
            all_here(sum_in.at[pl.ds(1, n_dp - 1)], all_sem.at[0])
            done[p] = piece_of(p)[...] + jnp.sum(sum_in[1:], axis=0)
            loop(1, n_dp, lambda k: done_copy(k, p).start())

    loop(1, n_seq, lambda k: col_copy(k).start())

    def store(n, head):
        cols = lanes_of(head, head_width)
        source, into = ((gated, gated_hbm), (query_grad, query_grad_hbm))[n]
        return pltpu.make_async_copy(source.at[:, cols], into.at[:, cols], store_sem.at[n])

    end_block = n_seq * blocks - 1

    def second_half(m):
        i, j, slot, head, cols = where_is(m)
        g = stack(grad, cols)
        prob = probs[i, pl.ds(pl.multiple_of(j * block, block), block), :]
        value = v_all[slot]
        attended = jnp.dot(prob, value, preferred_element_type=f32)
        prob_grad = lax.dot_general(g, value, NT, preferred_element_type=f32)
        gated[:, cols] = unstack((gate * attended).astype(bf16))
        delta = jnp.sum(g.astype(f32) * attended, axis=1, keepdims=True)
        score_grad = (prob.astype(f32) * (prob_grad - delta)).astype(bf16)
        out_grad = jnp.dot(score_grad, k_all[slot], preferred_element_type=f32)
        query_grad[:, cols] = unstack((out_grad * scale).astype(bf16))

        @pl.when(j == blocks - 1)
        def _():
            store(0, head).start()
            store(1, head).start()

        after_block(v_ways, m)
        pl.when(m == blocks - 1)(adapter_back)
        pl.when(m == min(3 * blocks - 1, end_block))(adapter_sum)
        pl.when(m == min(5 * blocks - 1, end_block))(adapter_done)

    loop(0, n_seq * blocks, second_half)

    loop(0, pieces, lambda j: pl.when(j != p)(lambda: done_copy(0, j).wait_recv()))
    for j in range(pieces - 2):
        r, c = 8 * (j % 2), LANES * (j // 2)
        fill = min(LANES, width - c)
        if fill > 0:
            down_stage[r : r + 8, c : c + fill] = done[j][:, :fill]
    up_stage[:8, :] = done[pieces - 2]
    up_stage[8:, :] = done[pieces - 1]
    store_down = pltpu.make_async_copy(down_stage, down_hbm, store_sem.at[2])
    store_up = pltpu.make_async_copy(up_stage, up_out_hbm, store_sem.at[3])
    store_down.start()
    store_up.start()

    most = pl.ds(0, n_seq - 1)
    all_sent(0, sum_k.at[most])
    all_sent(1, sum_v.at[most])
    all_sent(3, up_all.at[others])
    for n, out in enumerate((k_out, v_out, ext_out)):
        all_sent(4 + n, out.at[pl.ds(1, n_dp - 1)])
    all_sent(7, k_all.at[most])
    all_sent(8, v_all.at[most])
    all_sent(9, col_in.at[others])

    @pl.when(z == 0)
    def _():
        all_sent(10, back_in.at[pl.ds(1, n_dp - 1)])

    @pl.when(z != 0)
    def _():
        all_sent(10, back_in)

    @pl.when(p < pieces)
    def _():
        all_sent(11, sum_in.at[pl.ds(0, pieces - 1)])
        all_sent(12, sum_in.at[pl.ds(1, n_dp - 1)])

    @pl.when(p >= pieces)
    def _():
        all_sent(11, sum_in.at[pl.ds(0, pieces)])

    pltpu.make_async_copy(gated, gated_hbm, store_sem.at[0]).wait()
    pltpu.make_async_copy(query_grad, query_grad_hbm, store_sem.at[1]).wait()
    store_down.wait()
    store_up.wait()


def per_device(
    queries,
    output_gradient,
    tiles,
    frozen_key_weight,
    frozen_value_weight,
    key_norm_gain,
    adapter_down_weight,
    adapter_up_weight,
    gate,
    document_lengths,
    image_reader_group,
    image_document,
):
    n_dp, n_seq = lax.axis_size("dp"), lax.axis_size("seq")
    docs = document_lengths.shape[1]
    rank = adapter_up_weight.shape[0]
    img_dev, img_rows, width = tiles.shape
    rows = img_dev * img_rows
    tokens, columns = queries.shape
    keys = n_dp * img_rows
    block = min(HEADS_AT_ONCE * LANES, columns // n_seq) // LANES * tokens
    wide = -(-width // LANES) * LANES + LANES
    pieces = 2 * (wide // LANES)
    fit = LANES // img_rows
    any_space = pl.BlockSpec(memory_space=pl.ANY)
    f32, bf16 = jnp.float32, jnp.bfloat16

    def held(*shape, kind=bf16):
        return pltpu.VMEM(shape, kind)

    dma = pltpu.SemaphoreType.DMA
    gated, query_grad, down_rows, up_grad = pl.pallas_call(
        functools.partial(fused_kernel, n_dp, n_seq, docs),
        out_shape=(
            jax.ShapeDtypeStruct((tokens, columns), bf16),
            jax.ShapeDtypeStruct((tokens, columns), bf16),
            jax.ShapeDtypeStruct((rank, width), f32),
            jax.ShapeDtypeStruct((rank, LANES), f32),
        ),
        in_specs=[any_space] * 12,
        out_specs=(any_space,) * 4,
        scratch_shapes=[
            held(tokens, columns),
            held(tokens, columns),
            held(tokens, columns),
            held(tokens, columns),
            held(rows, width),
            held(width, n_seq * LANES),
            held(width, n_seq * LANES),
            held(rank, width),
            held(rank, LANES),
            held(1, LANES, kind=f32),
            pltpu.SMEM((1,), f32),
            pltpu.SMEM((1, docs), jnp.int32),
            pltpu.SMEM((img_dev,), jnp.int32),
            pltpu.SMEM((img_dev,), jnp.int32),
            held(2, rows, LANES, kind=f32),
            held(n_seq + 2, rows, LANES, kind=f32),
            held(n_seq + 2, rows, LANES),
            held(rank, rows, kind=f32),
            held(rank, rows),
            held(n_seq, rank, rows),
            held(n_seq, rank, LANES),
            pltpu.SMEM((n_dp,), jnp.int32),
            pltpu.SMEM((n_dp,), jnp.int32),
            held(img_dev, img_rows, LANES),
            held(img_dev, img_rows, LANES),
            held(img_dev, img_rows, LANES),
            held(n_dp, img_rows, LANES),
            held(n_dp, img_rows, LANES),
            held(n_dp, img_rows, LANES),
            held(n_seq, keys, LANES),
            held(n_seq, keys, LANES),
            held(keys, LANES),
            held(LANES, keys),
            held(block, LANES),
            held(n_seq, columns // n_seq // LANES * tokens, keys),
            held(LANES, keys, kind=f32),
            held(2 * rank, keys, kind=f32),
            held(n_seq, 2 * rank, LANES, kind=f32),
            held(fit, rank, LANES),
            held(n_dp, rank, LANES),
            held(rank, wide, kind=f32),
            held(n_dp, 8, LANES, kind=f32),
            held(pieces, 8, LANES, kind=f32),
            held(rank, width, kind=f32),
            held(rank, LANES, kind=f32),
            dma((12,)),
            dma((4,)),
            dma((13,)),
            dma((5,)),
            dma((2, 2, n_seq // 2, PARTS)),
            dma((3, PARTS)),
            dma((4, n_seq // 2, PARTS)),
            dma((pieces,)),
        ],
        compiler_params=pltpu.CompilerParams(
            collective_id=0, has_side_effects=True, vmem_limit_bytes=58 << 20
        ),
    )(
        queries,
        output_gradient,
        tiles.reshape(rows, width),
        frozen_key_weight,
        frozen_value_weight,
        adapter_down_weight.T,
        adapter_up_weight,
        key_norm_gain.reshape(1, -1),
        gate,
        document_lengths,
        image_reader_group,
        image_document,
    )
    return (gated, query_grad, down_rows.T, up_grad)


def solution(mesh):
    placed = (
        P(("dp", "seq"), None),
        P(("dp", "seq"), None),
        P("dp", None, "seq"),
        P("seq", None),
        P("seq", None),
        P(),
        P("seq", None),
        P(None, "seq"),
        P(),
        P("dp", None),
        P("dp"),
        P("dp"),
    )
    return jax.shard_map(
        per_device,
        mesh=mesh,
        in_specs=placed,
        out_specs=(P(("dp", "seq"), None), P(("dp", "seq"), None), P("seq", None), P(None, "seq")),
        check_vma=False,
    )
```

```python
import functools

import jax
import jax.numpy as jnp
from jax import lax
from jax.experimental import pallas as pl
from jax.experimental.pallas import tpu as pltpu
from jax.sharding import PartitionSpec as P

EPS = 1e-05
ADAPTER_SCALE = 2.0
MASKED = -1e30
LANES = 128
PARTS = 4
HEADS_AT_ONCE = 4
EVENTS = (2, 6, 10)
LOG2_E = 1.4426950408889634
MESH = pl.DeviceIdType.MESH
NT = (((1,), (1,)), ((), ()))
TN = (((0,), (0,)), ((), ()))


def remote(src, dst, send_sem, recv_sem, target):
    return pltpu.make_async_remote_copy(
        src_ref=src,
        dst_ref=dst,
        send_sem=send_sem,
        recv_sem=recv_sem,
        device_id=target,
        device_id_type=MESH,
    )


def loop(first, last, body):
    def step(i, carry):
        body(i)
        return carry

    lax.fori_loop(first, last, step, 0)


def greet(barrier, target):
    pl.semaphore_signal(barrier, inc=1, device_id=target, device_id_type=MESH)


def stages_of(n_dp):
    stages, stride = [], 1
    while stride < n_dp:
        size = min(8, n_dp // stride)
        stages.append((stride, size))
        stride *= size
    return stages


def fused_kernel(
    n_dp,
    n_seq,
    docs,
    stages,
    query_hbm,
    grad_hbm,
    tiles_hbm,
    wk_hbm,
    wv_hbm,
    wd_hbm,
    up_hbm,
    gain_hbm,
    gate_hbm,
    length_hbm,
    reader_hbm,
    doc_hbm,
    gated_hbm,
    query_grad_hbm,
    down_hbm,
    up_out_hbm,
    query,
    grad,
    gated,
    query_grad,
    tiles,
    wk,
    wv,
    wd,
    up,
    gain,
    gate_s,
    lengths,
    reader,
    doc,
    own,
    sum_k,
    sum_v,
    low_own,
    low_out,
    low_in,
    up_all,
    pick,
    tag,
    rows_k,
    rows_v,
    ext_rows,
    k_out,
    v_out,
    ext_out,
    k_all,
    v_all,
    ext,
    ext_t,
    bias,
    probs,
    value_grad,
    small,
    col_in,
    back_out,
    back_in,
    total,
    stage_out,
    stage_in,
    down_stage,
    up_stage,
    load_sem,
    store_sem,
    sent_sem,
    all_sem,
    sum_sem,
    route_sem,
    ring_sem,
    stage_sem,
):
    p = lax.axis_index("dp")
    z = lax.axis_index("seq")
    rows, width = tiles.shape
    tokens, columns = query.shape
    rank = up.shape[0]
    img_dev, img_rows = rows_k.shape[:2]
    keys = ext.shape[0]
    head_width = columns // n_seq
    block = bias.shape[0]
    span = (block // tokens) * LANES
    blocks = head_width // span
    fit = LANES // img_rows
    half = rows // 2
    mid = n_seq // 2
    sum_rows = rows // PARTS
    scale = LANES ** (-0.5)
    f32, bf16 = jnp.float32, jnp.bfloat16
    right = (p, lax.rem(z + 1, n_seq))
    left = (p, lax.rem(z + n_seq - 1, n_seq))

    def lanes_of(n, size=LANES):
        return pl.ds(pl.multiple_of(n * size, size), size)

    def load(n, source, into):
        return pltpu.make_async_copy(source, into, load_sem.at[n])

    load_tiles, load_wk = load(0, tiles_hbm, tiles), load(1, wk_hbm, wk)
    load_wv, load_wd = load(2, wv_hbm, wv), load(3, wd_hbm, wd)
    load_up, load_gain = load(4, up_hbm, up), load(5, gain_hbm, gain)
    load_gate, load_lengths = load(6, gate_hbm, gate_s), load(7, length_hbm, lengths)
    load_reader, load_doc = load(8, reader_hbm, reader), load(9, doc_hbm, doc)
    load_query, load_grad = load(10, query_hbm, query), load(11, grad_hbm, grad)
    for copy in (load_tiles, load_wk, load_wd, load_up, load_gain, load_gate, load_lengths):
        copy.start()
    for copy in (load_reader, load_doc, load_wv):
        copy.start()
    barrier = pltpu.get_barrier_semaphore()
    loop(1, n_seq, lambda k: greet(barrier, (p, lax.rem(z + k, n_seq))))
    loop(1, n_dp, lambda k: greet(barrier, (lax.rem(p + k, n_dp), z)))

    def greet_back(k):
        @pl.when((k != 0) | (z != 0))
        def _():
            greet(barrier, (lax.rem(p + k, n_dp), k // fit))

    loop(0, n_dp, greet_back)

    def all_sent(n, region):
        remote(region, region, sent_sem.at[n], all_sem.at[0], right).wait_send()

    def all_here(region, sem):
        remote(region, region, sent_sem.at[0], sem, right).wait_recv()

    def in_part(b):
        return pl.ds(b * sum_rows, sum_rows)

    def goes(side, b):
        return (b < PARTS // 2) == (side == 0)

    def hop(n, side, t, b):
        sums = (sum_k, sum_v)[n]
        at = side * (mid + 1) + t
        return remote(
            sums.at[at, in_part(b)],
            sums.at[at + 1, in_part(b)],
            sent_sem.at[n],
            sum_sem.at[n, side, t, b],
            (right, left)[side],
        )

    def own_part(n, head):
        weight = (wk, wv)[n]
        return jnp.dot(tiles[...], weight[:, lanes_of(head)], preferred_element_type=f32)

    def first_sums(n):
        sums = (sum_k, sum_v)[n]
        part = own_part(n, lax.rem(z + mid, n_seq)).astype(sums.dtype)
        sums[0, :half, :] = part[:half]
        sums[mid + 1, half:, :] = part[half:]

    def first_sends(n):
        for b in range(PARTS):
            hop(n, 0 if goes(0, b) else 1, 0, b).start()

    def sum_step(n, t):
        sums = (sum_k, sum_v)[n]
        own[0] = own_part(n, lax.rem(z + mid - t, n_seq))
        own[1] = own_part(n, lax.rem(z + mid + t, n_seq))
        for c in range(PARTS):
            for side in (0, 1):
                b = c if side == 0 else (c + PARTS // 2) % PARTS
                at = side * (mid + 1) + t
                total_here = own[side, in_part(b), :]
                if t > 1 or goes(side, b):
                    hop(n, side, t - 1, b).wait_recv()
                    total_here = total_here + sums[at, in_part(b), :].astype(f32)
                sums[at, in_part(b), :] = total_here.astype(sums.dtype)
                hop(n, side, t, b).start()

    def last_sums(n, b):
        sums = (sum_k, sum_v)[n]
        total_here = own[0, in_part(b), :]
        for side in (0, 1):
            if mid > 1 or goes(side, b):
                hop(n, side, mid - 1, b).wait_recv()
                at = side * (mid + 1) + mid
                total_here = total_here + sums[at, in_part(b), :].astype(f32)
        return total_here

    load_tiles.wait()
    load_wk.wait()
    first_sums(0)
    pl.semaphore_wait(barrier, n_seq - 1 + n_dp - 1 + n_dp - jnp.where(z == 0, 1, 0))
    first_sends(0)

    def low_copy(k):
        target = (p, lax.rem(z + k, n_seq))
        return remote(low_out, low_in.at[k], sent_sem.at[2], all_sem.at[1], target)

    def up_copy(k):
        target = (p, lax.rem(z + k, n_seq))
        return remote(up, up_all.at[k], sent_sem.at[3], all_sem.at[2], target)

    others = pl.ds(1, n_seq - 1)

    load_wd.wait()
    load_up.wait()
    low_own[...] = lax.dot_general(wd[...], tiles[...], NT, preferred_element_type=f32)
    low_out[...] = low_own[...].astype(bf16)
    loop(1, n_seq, lambda k: low_copy(k).start())
    loop(1, n_seq, lambda k: up_copy(k).start())
    up_all[0] = up[...]
    load_query.start()
    load_grad.start()
    for copy in (load_gain, load_gate, load_lengths, load_reader, load_doc):
        copy.wait()

    def find(g):
        at, mark = jnp.int32(0), jnp.int32(docs)
        for i in range(img_dev):
            hit = reader[i] == g
            at = jnp.where(hit, i, at)
            mark = jnp.where(hit, doc[i], mark)
        pick[g] = at
        tag[g] = mark

    loop(0, n_dp, find)

    part_rows = keys // PARTS
    slots = n_dp // PARTS

    def routed(n, into, b):
        skip = img_rows if b == 0 else 0
        part = into.at[pl.ds(b * part_rows + skip, part_rows - skip)]
        all_here(part, route_sem.at[n, b])

    def route(n, out, into, k):
        g = lax.rem(p + k, n_dp)
        return remote(
            out.at[k],
            into.at[pl.ds(pl.multiple_of(k * img_rows, img_rows), img_rows)],
            sent_sem.at[4 + n],
            route_sem.at[n, k // slots],
            (g, z),
        )

    def k_route(k):
        return route(0, k_out, k_all.at[0], k)

    def v_route(k):
        return route(1, v_out, v_all.at[0], k)

    def ext_route(k):
        return route(2, ext_out, ext, k)

    lane = lax.broadcasted_iota(jnp.int32, (img_rows, LANES), 1)

    def ext_block(g):
        mark = jnp.where(lane == rank + tag[g], 1.0, 0.0)
        low = ext_rows[pick[g]].astype(f32)
        return jnp.where(lane < rank, low, mark).astype(bf16)

    def send_ext(k):
        ext_out[k] = ext_block(lax.rem(p + k, n_dp))
        ext_route(k).start()

    def low_finish():
        all_sent(2, low_in.at[others])
        all_here(low_in.at[others], all_sem.at[1])
        low_total = low_own[...]
        for k in range(1, n_seq):
            low_total = low_total + low_in[k].astype(f32)
        low_rank = low_total.astype(bf16)
        low_out[...] = low_rank
        eye = lax.broadcasted_iota(jnp.int32, (rank, LANES), 0) == lax.broadcasted_iota(
            jnp.int32, (rank, LANES), 1
        )
        eye = jnp.where(eye, 1.0, 0.0).astype(bf16)
        low_rows = lax.dot_general(low_rank, eye, TN, preferred_element_type=f32)
        ext_rows[...] = low_rows.astype(bf16).reshape(img_dev, img_rows, LANES)

    for t in range(1, mid):
        if t == mid - 1:
            low_finish()
            loop(1, n_dp, send_ext)
            load_wv.wait()
            first_sums(1)
            first_sends(1)
        sum_step(0, t)
    if mid == 1:
        low_finish()
        loop(1, n_dp, send_ext)
        load_wv.wait()
        first_sums(1)
        first_sends(1)

    per_part = sum_rows // img_rows
    own[0] = own_part(0, z)
    for b in range(PARTS):
        key_raw = last_sums(0, b)
        mean_square = jnp.mean(key_raw * key_raw, axis=-1, keepdims=True)
        key_rows = (key_raw * lax.rsqrt(mean_square + EPS) * gain[...]).astype(bf16)
        rows_k[pl.ds(b * per_part, per_part)] = key_rows.reshape(per_part, img_rows, LANES)

    def send_k(k):
        k_out[k] = rows_k[pick[lax.rem(p + k, n_dp)]]
        k_route(k).start()

    loop(1, n_dp, send_k)
    k_all[0, :img_rows, :] = rows_k[pick[p]]
    ext[:img_rows, :] = ext_block(p)

    lane_tok = lax.broadcasted_iota(jnp.int32, (tokens, LANES), 1)
    place = lax.broadcasted_iota(jnp.int32, (tokens, LANES), 0) + z * tokens
    own_doc = jnp.zeros((tokens, LANES), jnp.int32)
    end = jnp.int32(0)
    for d in range(docs - 1):
        end = end + lengths[0, d]
        own_doc = own_doc + jnp.where(place >= end, 1, 0)
    other = (lane_tok >= rank) & (lane_tok <= rank + docs) & (lane_tok != rank + own_doc)
    penalty = jnp.where(other, MASKED, 0.0).astype(bf16)
    for n in range(block // tokens):
        bias[n * tokens : (n + 1) * tokens, :] = penalty
    small[...] = jnp.zeros_like(small)
    gate = jnp.tanh(jnp.full((1, LANES), gate_s[0], f32))
    all_here(up_all.at[others], all_sem.at[2])
    for b in range(PARTS):
        routed(2, ext, b)
    ext_t[...] = ext[...].T
    load_query.wait()
    load_grad.wait()

    for t in range(1, mid):
        sum_step(1, t)
    last = mid - 1

    def gather(held, n):
        def ahead(t, b):
            part = pl.ds(pl.multiple_of(b * part_rows, part_rows), part_rows)
            source, into = lax.rem(n_seq - t, n_seq), n_seq - 1 - t
            return remote(
                held.at[source, part],
                held.at[into, part],
                sent_sem.at[7 + n // 2],
                ring_sem.at[n, t, b],
                right,
            )

        def back(t, b):
            part = pl.ds(pl.multiple_of(b * part_rows, part_rows), part_rows)
            return remote(
                held.at[t, part],
                held.at[t + 1, part],
                sent_sem.at[7 + n // 2],
                ring_sem.at[n + 1, t, b],
                left,
            )

        return ((ahead, lambda b: b < PARTS // 2), (back, lambda b: b >= PARTS // 2))

    k_ways, v_ways = gather(k_all, 0), gather(v_all, 2)

    def gather_start(ways, n, held):
        for b in range(PARTS):
            routed(n, held.at[0], b)
            for way, whole in ways:
                if last > 0 or whole(b):
                    way(0, b).start()

    def forward(ways, t, b):
        for way, whole in ways:

            @pl.when((t <= last) | whole(b))
            def _():
                way(t - 1, b).wait_recv()

            @pl.when((t < last) | ((t == last) & whole(b)))
            def _():
                way(t, b).start()

    def after_block(ways, m, first_head):
        i = m // blocks
        step = (i + 1) // 2
        q = m - blocks * (2 * step - 1)
        per = PARTS // (2 * blocks)

        pl.when(m == blocks - 1)(first_head)

        @pl.when((i >= 1) & (i < n_seq - 1))
        def _():
            loop(q * per, (q + 1) * per, lambda b: forward(ways, step + 1, b))


    def send_v(k):
        v_out[k] = rows_v[pick[lax.rem(p + k, n_dp)]]
        v_route(k).start()

    def values_out():
        low_up = lax.dot_general(low_out[...], up[...], TN, preferred_element_type=f32)
        own[0] = own_part(1, z) + ADAPTER_SCALE * low_up
        for b in range(PARTS):
            value = last_sums(1, b).astype(bf16)
            rows_v[pl.ds(b * per_part, per_part)] = value.reshape(per_part, img_rows, LANES)
        v_all[0, :img_rows, :] = rows_v[pick[p]]
        for b in range(PARTS):
            forward(k_ways, 1, b)
            loop(max(1, b * slots), (b + 1) * slots, send_v)

    def values_on():
        loop(0, PARTS, lambda b: forward(v_ways, 1, b))

    def stack(ref, cols):
        part = ref[:, cols]
        return jnp.concatenate(
            [part[:, n * LANES : (n + 1) * LANES] for n in range(block // tokens)], axis=0
        )

    def unstack(x):
        return jnp.concatenate(
            [x[n * tokens : (n + 1) * tokens] for n in range(block // tokens)], axis=1
        )

    def where_is(m):
        i, j = m // blocks, lax.rem(m, blocks)
        slot = jnp.where(lax.rem(i, 2) == 1, n_seq - (i + 1) // 2, i // 2)
        head = lax.rem(z + slot, n_seq)
        cols = pl.ds(pl.multiple_of(head * head_width + j * span, span), span)
        return i, j, slot, head, cols

    def first_half(m):
        i, j, slot, head, cols = where_is(m)
        g = (gate * stack(grad, cols).astype(f32)).astype(bf16)
        grad[:, cols] = unstack(g)
        q = jnp.concatenate([stack(query, cols), bias[...]], axis=1)
        key_ext = jnp.concatenate([k_all[slot], ext[...]], axis=1)
        scores = lax.dot_general(q, key_ext, NT, preferred_element_type=f32)
        row_max = jnp.max(scores, axis=1, keepdims=True)
        weights = jnp.exp2((scores - row_max) * (scale * LOG2_E))
        prob = weights * (1.0 / jnp.sum(weights, axis=1, keepdims=True))
        prob = prob.astype(bf16)
        probs[i, pl.ds(pl.multiple_of(j * block, block), block), :] = prob
        part = lax.dot_general(g, prob, TN, preferred_element_type=f32)

        @pl.when(j == 0)
        def _():
            value_grad[...] = part

        @pl.when(j > 0)
        def _():
            value_grad[...] += part

        @pl.when(j == blocks - 1)
        def _():
            whole = value_grad[...].astype(bf16)
            small[:rank, :] += jnp.dot(
                up_all[lax.rem(n_seq - slot, n_seq)], whole, preferred_element_type=f32
            )
            small[rank:, lanes_of(head)] = lax.dot_general(
                ext_t[:rank, :], whole, NT, preferred_element_type=f32
            )

        after_block(k_ways, m, values_out)

        @pl.when(m == max(blocks * (2 * last - 1), blocks) - 1)
        def _():
            gather_start(v_ways, 1, v_all)

    gather_start(k_ways, 0, k_all)
    loop(0, n_seq * blocks, first_half)

    def col_copy(k):
        target = lax.rem(z + k, n_seq)
        return remote(
            small.at[:, lanes_of(target)], col_in.at[k], sent_sem.at[9], all_sem.at[3], (p, target)
        )

    wide = total.shape[1]

    def back_copy(n):
        j, s = lax.rem(n, fit), n // fit
        o = lax.rem(p + n_dp - fit * z - j, n_dp)
        into = back_in.at[fit * z + j]
        return remote(back_out.at[j], into, sent_sem.at[10], all_sem.at[4], (o, s))

    def stage_copy(r, k, send):
        stride, size = stages[r]
        digit = lax.rem(p // stride, size)
        peer = lax.rem(digit + k, size)
        slot = digit if send else lax.rem(digit + size - k, size)
        return remote(
            stage_out[r],
            stage_in[r].at[slot],
            sent_sem.at[12 + r],
            stage_sem.at[r, k],
            (p + (peer - digit) * stride, z),
        )

    def stage_start(r):
        stride, size = stages[r]
        stage_out[r][...] = total[...].astype(bf16)
        stage_in[r][lax.rem(p // stride, size)] = stage_out[r][...]
        for k in range(1, size):
            stage_copy(r, k, True).start()

    def stage_finish(r):
        size = stages[r][1]
        for k in range(1, size):
            stage_copy(r, k, False).wait_recv()
        here = stage_in[r][0].astype(f32)
        for d in range(1, size):
            here = here + stage_in[r][d].astype(f32)
        total[...] = here
        if r + 1 < len(stages):
            stage_start(r + 1)

    def adapter_back():
        mine = small[:, lanes_of(z)]
        all_here(col_in.at[others], all_sem.at[3])
        for k in range(1, n_seq):
            mine = mine + col_in[k]
        mine = ADAPTER_SCALE * mine
        for j in range(fit):
            moved = mine[:rank]
            if j > 0:
                moved = pltpu.roll(moved, LANES - j * img_rows, 1)
            back_out[j] = moved.astype(bf16)
        total[:, width:] = jnp.zeros((rank, wide - width), f32)
        total[:, wide - LANES :] = mine[rank:]
        loop(1, fit * n_seq, lambda n: back_copy(n).start())

        @pl.when(z == 0)
        def _():
            back_in[0] = back_out[0]

        @pl.when(z != 0)
        def _():
            back_copy(0).start()

    def adapter_sum():
        @pl.when(z == 0)
        def _():
            all_here(back_in.at[pl.ds(1, n_dp - 1)], all_sem.at[4])

        @pl.when(z != 0)
        def _():
            all_here(back_in, all_sem.at[4])

        lane_rank = lax.broadcasted_iota(jnp.int32, (rank, LANES), 1)
        pieces_in = []
        for first in range(0, img_dev, fit):
            piece = jnp.zeros((rank, LANES), f32)
            for i in range(fit):
                slot = lax.rem(reader[first + i] - p + n_dp, n_dp)
                held = back_in[slot].astype(f32)
                if i > 0:
                    held = pltpu.roll(held, i * img_rows, 1)
                piece = jnp.where(lane_rank // img_rows == i, held, piece)
            pieces_in.append(piece.astype(bf16))
        total[:, :width] = jnp.dot(
            jnp.concatenate(pieces_in, axis=1), tiles[...], preferred_element_type=f32
        )
        stage_start(0)

    loop(1, n_seq, lambda k: col_copy(k).start())

    def store(n, head):
        cols = lanes_of(head, head_width)
        source, into = ((gated, gated_hbm), (query_grad, query_grad_hbm))[n]
        return pltpu.make_async_copy(source.at[:, cols], into.at[:, cols], store_sem.at[n])

    end_block = n_seq * blocks - 1

    def second_half(m):
        i, j, slot, head, cols = where_is(m)
        g = stack(grad, cols)
        prob = probs[i, pl.ds(pl.multiple_of(j * block, block), block), :]
        value = v_all[slot]
        attended = jnp.dot(prob, value, preferred_element_type=f32)
        prob_grad = lax.dot_general(g, value, NT, preferred_element_type=f32)
        gated[:, cols] = unstack((gate * attended).astype(bf16))
        delta = jnp.sum(g.astype(f32) * attended, axis=1, keepdims=True)
        score_grad = (prob.astype(f32) * (prob_grad - delta)).astype(bf16)
        out_grad = jnp.dot(score_grad, k_all[slot], preferred_element_type=f32)
        query_grad[:, cols] = unstack((out_grad * scale).astype(bf16))

        @pl.when(j == blocks - 1)
        def _():
            store(0, head).start()
            store(1, head).start()

        after_block(v_ways, m, values_on)
        events = [adapter_back, adapter_sum]
        events += [functools.partial(stage_finish, r) for r in range(len(stages) - 1)]
        for at, event in zip(EVENTS, events):
            pl.when(m == min(at, end_block))(event)

    loop(0, n_seq * blocks, second_half)

    stage_finish(len(stages) - 1)
    down_stage[...] = total[:, :width]
    up_stage[...] = total[:, wide - LANES :]
    store_down = pltpu.make_async_copy(down_stage, down_hbm, store_sem.at[2])
    store_up = pltpu.make_async_copy(up_stage, up_out_hbm, store_sem.at[3])
    store_down.start()
    store_up.start()

    most = pl.ds(0, n_seq - 1)
    all_sent(0, sum_k.at[most])
    all_sent(1, sum_v.at[most])
    all_sent(3, up_all.at[others])
    for n, out in enumerate((k_out, v_out, ext_out)):
        all_sent(4 + n, out.at[pl.ds(1, n_dp - 1)])
    all_sent(7, k_all.at[most])
    all_sent(8, v_all.at[most])
    all_sent(9, col_in.at[others])

    @pl.when(z == 0)
    def _():
        all_sent(10, back_in.at[pl.ds(1, n_dp - 1)])

    @pl.when(z != 0)
    def _():
        all_sent(10, back_in)

    for r, (stride, size) in enumerate(stages):
        all_sent(12 + r, stage_in[r].at[pl.ds(0, size - 1)])
    pltpu.make_async_copy(gated, gated_hbm, store_sem.at[0]).wait()
    pltpu.make_async_copy(query_grad, query_grad_hbm, store_sem.at[1]).wait()
    store_down.wait()
    store_up.wait()


def per_device(
    queries,
    output_gradient,
    tiles,
    frozen_key_weight,
    frozen_value_weight,
    key_norm_gain,
    adapter_down_weight,
    adapter_up_weight,
    gate,
    document_lengths,
    image_reader_group,
    image_document,
):
    n_dp, n_seq = lax.axis_size("dp"), lax.axis_size("seq")
    docs = document_lengths.shape[1]
    rank = adapter_up_weight.shape[0]
    img_dev, img_rows, width = tiles.shape
    rows = img_dev * img_rows
    tokens, columns = queries.shape
    keys = n_dp * img_rows
    block = min(HEADS_AT_ONCE * LANES, columns // n_seq) // LANES * tokens
    wide = -(-width // LANES) * LANES + LANES
    stages = stages_of(n_dp)
    fit = LANES // img_rows
    any_space = pl.BlockSpec(memory_space=pl.ANY)
    f32, bf16 = jnp.float32, jnp.bfloat16

    def held(*shape, kind=bf16):
        return pltpu.VMEM(shape, kind)

    dma = pltpu.SemaphoreType.DMA
    gated, query_grad, down_rows, up_grad = pl.pallas_call(
        functools.partial(fused_kernel, n_dp, n_seq, docs, stages),
        out_shape=(
            jax.ShapeDtypeStruct((tokens, columns), bf16),
            jax.ShapeDtypeStruct((tokens, columns), bf16),
            jax.ShapeDtypeStruct((rank, width), f32),
            jax.ShapeDtypeStruct((rank, LANES), f32),
        ),
        in_specs=[any_space] * 12,
        out_specs=(any_space,) * 4,
        scratch_shapes=[
            held(tokens, columns),
            held(tokens, columns),
            held(tokens, columns),
            held(tokens, columns),
            held(rows, width),
            held(width, n_seq * LANES),
            held(width, n_seq * LANES),
            held(rank, width),
            held(rank, LANES),
            held(1, LANES, kind=f32),
            pltpu.SMEM((1,), f32),
            pltpu.SMEM((1, docs), jnp.int32),
            pltpu.SMEM((img_dev,), jnp.int32),
            pltpu.SMEM((img_dev,), jnp.int32),
            held(2, rows, LANES, kind=f32),
            held(n_seq + 2, rows, LANES, kind=f32),
            held(n_seq + 2, rows, LANES),
            held(rank, rows, kind=f32),
            held(rank, rows),
            held(n_seq, rank, rows),
            held(n_seq, rank, LANES),
            pltpu.SMEM((n_dp,), jnp.int32),
            pltpu.SMEM((n_dp,), jnp.int32),
            held(img_dev, img_rows, LANES),
            held(img_dev, img_rows, LANES),
            held(img_dev, img_rows, LANES),
            held(n_dp, img_rows, LANES),
            held(n_dp, img_rows, LANES),
            held(n_dp, img_rows, LANES),
            held(n_seq, keys, LANES),
            held(n_seq, keys, LANES),
            held(keys, LANES),
            held(LANES, keys),
            held(block, LANES),
            held(n_seq, columns // n_seq // LANES * tokens, keys),
            held(LANES, keys, kind=f32),
            held(2 * rank, keys, kind=f32),
            held(n_seq, 2 * rank, LANES, kind=f32),
            held(fit, rank, LANES),
            held(n_dp, rank, LANES),
            held(rank, wide, kind=f32),
            [held(rank, wide) for stage in stages],
            [held(size, rank, wide) for stride, size in stages],
            held(rank, width, kind=f32),
            held(rank, LANES, kind=f32),
            dma((12,)),
            dma((4,)),
            dma((15,)),
            dma((6,)),
            dma((2, 2, n_seq // 2, PARTS)),
            dma((3, PARTS)),
            dma((4, n_seq // 2, PARTS)),
            dma((len(stages), 8)),
        ],
        compiler_params=pltpu.CompilerParams(
            collective_id=0, has_side_effects=True, vmem_limit_bytes=58 << 20
        ),
    )(
        queries,
        output_gradient,
        tiles.reshape(rows, width),
        frozen_key_weight,
        frozen_value_weight,
        adapter_down_weight.T,
        adapter_up_weight,
        key_norm_gain.reshape(1, -1),
        gate,
        document_lengths,
        image_reader_group,
        image_document,
    )
    return (gated, query_grad, down_rows.T, up_grad)


def solution(mesh):
    placed = (
        P(("dp", "seq"), None),
        P(("dp", "seq"), None),
        P("dp", None, "seq"),
        P("seq", None),
        P("seq", None),
        P(),
        P("seq", None),
        P(None, "seq"),
        P(),
        P("dp", None),
        P("dp"),
        P("dp"),
    )
    return jax.shard_map(
        per_device,
        mesh=mesh,
        in_specs=placed,
        out_specs=(P(("dp", "seq"), None), P(("dp", "seq"), None), P("seq", None), P(None, "seq")),
        check_vma=False,
    )
```

```python
import functools

import jax
import jax.numpy as jnp
from jax import lax
from jax.experimental import pallas as pl
from jax.experimental.pallas import tpu as pltpu
from jax.sharding import PartitionSpec as P

EPS = 1e-05
ADAPTER_SCALE = 2.0
MASKED = -1e30
LANES = 128
PARTS = 4
HEADS_AT_ONCE = 4
EVENTS = (2, 6, 10)
LOG2_E = 1.4426950408889634
MESH = pl.DeviceIdType.MESH
NT = (((1,), (1,)), ((), ()))
TN = (((0,), (0,)), ((), ()))


def remote(src, dst, send_sem, recv_sem, target):
    return pltpu.make_async_remote_copy(
        src_ref=src,
        dst_ref=dst,
        send_sem=send_sem,
        recv_sem=recv_sem,
        device_id=target,
        device_id_type=MESH,
    )


def loop(first, last, body):
    def step(i, carry):
        body(i)
        return carry

    lax.fori_loop(first, last, step, 0)


def greet(barrier, target):
    pl.semaphore_signal(barrier, inc=1, device_id=target, device_id_type=MESH)


def stages_of(n_dp):
    stages, stride = [], 1
    while stride < n_dp:
        size = min(8, n_dp // stride)
        stages.append((stride, size))
        stride *= size
    return stages


def fused_kernel(
    n_dp,
    n_seq,
    docs,
    stages,
    query_hbm,
    grad_hbm,
    tiles_hbm,
    wk_hbm,
    wv_hbm,
    wd_hbm,
    up_hbm,
    gain_hbm,
    gate_hbm,
    length_hbm,
    reader_hbm,
    doc_hbm,
    gated_hbm,
    query_grad_hbm,
    down_hbm,
    up_out_hbm,
    query,
    grad,
    gated,
    query_grad,
    tiles,
    wk,
    wv,
    wd,
    up,
    gain,
    gate_s,
    lengths,
    reader,
    doc,
    own,
    sum_k,
    sum_v,
    low_own,
    low_out,
    low_in,
    up_all,
    pick,
    tag,
    rows_k,
    rows_v,
    ext_rows,
    k_out,
    v_out,
    ext_out,
    k_all,
    v_all,
    ext,
    ext_t,
    bias,
    probs,
    value_grad,
    small,
    col_in,
    back_out,
    back_in,
    total,
    stage_out,
    stage_in,
    down_stage,
    up_stage,
    load_sem,
    store_sem,
    sent_sem,
    all_sem,
    sum_sem,
    route_sem,
    ring_sem,
    stage_sem,
):
    p = lax.axis_index("dp")
    z = lax.axis_index("seq")
    rows, width = tiles.shape
    tokens, columns = query.shape
    rank = up.shape[0]
    img_dev, img_rows = rows_k.shape[:2]
    keys = ext.shape[0]
    head_width = columns // n_seq
    block = bias.shape[0]
    span = (block // tokens) * LANES
    blocks = head_width // span
    fit = LANES // img_rows
    half = rows // 2
    mid = n_seq // 2
    sum_rows = rows // PARTS
    scale = LANES ** (-0.5)
    f32, bf16 = jnp.float32, jnp.bfloat16
    right = (p, lax.rem(z + 1, n_seq))
    left = (p, lax.rem(z + n_seq - 1, n_seq))

    def lanes_of(n, size=LANES):
        return pl.ds(pl.multiple_of(n * size, size), size)

    def load(n, source, into):
        return pltpu.make_async_copy(source, into, load_sem.at[n])

    load_tiles, load_wk = load(0, tiles_hbm, tiles), load(1, wk_hbm, wk)
    load_wv, load_wd = load(2, wv_hbm, wv), load(3, wd_hbm, wd)
    load_up, load_gain = load(4, up_hbm, up), load(5, gain_hbm, gain)
    load_gate, load_lengths = load(6, gate_hbm, gate_s), load(7, length_hbm, lengths)
    load_reader, load_doc = load(8, reader_hbm, reader), load(9, doc_hbm, doc)
    load_query, load_grad = load(10, query_hbm, query), load(11, grad_hbm, grad)
    for copy in (load_tiles, load_wk, load_wd, load_up, load_gain, load_gate, load_lengths):
        copy.start()
    for copy in (load_reader, load_doc, load_wv):
        copy.start()
    barrier = pltpu.get_barrier_semaphore()
    loop(1, n_seq, lambda k: greet(barrier, (p, lax.rem(z + k, n_seq))))
    loop(1, n_dp, lambda k: greet(barrier, (lax.rem(p + k, n_dp), z)))

    def greet_back(k):
        @pl.when((k != 0) | (z != 0))
        def _():
            greet(barrier, (lax.rem(p + k, n_dp), k // fit))

    loop(0, n_dp, greet_back)

    def all_sent(n, region):
        remote(region, region, sent_sem.at[n], all_sem.at[0], right).wait_send()

    def all_here(region, sem):
        remote(region, region, sent_sem.at[0], sem, right).wait_recv()

    def in_part(b):
        return pl.ds(b * sum_rows, sum_rows)

    def goes(side, b):
        return (b < PARTS // 2) == (side == 0)

    def hop(n, side, t, b):
        sums = (sum_k, sum_v)[n]
        at = side * (mid + 1) + t
        return remote(
            sums.at[at, in_part(b)],
            sums.at[at + 1, in_part(b)],
            sent_sem.at[n],
            sum_sem.at[n, side, t, b],
            (right, left)[side],
        )

    def own_part(n, head):
        weight = (wk, wv)[n]
        return jnp.dot(tiles[...], weight[:, lanes_of(head)], preferred_element_type=f32)

    def first_sums(n):
        sums = (sum_k, sum_v)[n]
        part = own_part(n, lax.rem(z + mid, n_seq)).astype(sums.dtype)
        sums[0, :half, :] = part[:half]
        sums[mid + 1, half:, :] = part[half:]

    def first_sends(n):
        for b in range(PARTS):
            hop(n, 0 if goes(0, b) else 1, 0, b).start()

    def sum_step(n, t):
        sums = (sum_k, sum_v)[n]
        own[0] = own_part(n, lax.rem(z + mid - t, n_seq))
        own[1] = own_part(n, lax.rem(z + mid + t, n_seq))
        for c in range(PARTS):
            for side in (0, 1):
                b = (c + PARTS // 2) % PARTS if side == 0 else c
                at = side * (mid + 1) + t
                total_here = own[side, in_part(b), :]
                if t > 1 or goes(side, b):
                    hop(n, side, t - 1, b).wait_recv()
                    total_here = total_here + sums[at, in_part(b), :].astype(f32)
                sums[at, in_part(b), :] = total_here.astype(sums.dtype)
                hop(n, side, t, b).start()

    def last_sums(n, b):
        sums = (sum_k, sum_v)[n]
        total_here = own[0, in_part(b), :]
        for side in (0, 1):
            if mid > 1 or goes(side, b):
                hop(n, side, mid - 1, b).wait_recv()
                at = side * (mid + 1) + mid
                total_here = total_here + sums[at, in_part(b), :].astype(f32)
        return total_here

    load_tiles.wait()
    load_wk.wait()
    first_sums(0)
    pl.semaphore_wait(barrier, n_seq - 1 + n_dp - 1 + n_dp - jnp.where(z == 0, 1, 0))
    first_sends(0)

    def low_copy(k):
        target = (p, lax.rem(z + k, n_seq))
        return remote(low_out, low_in.at[k], sent_sem.at[2], all_sem.at[1], target)

    def up_copy(k):
        target = (p, lax.rem(z + k, n_seq))
        return remote(up, up_all.at[k], sent_sem.at[3], all_sem.at[2], target)

    others = pl.ds(1, n_seq - 1)

    load_wd.wait()
    load_up.wait()
    low_own[...] = lax.dot_general(wd[...], tiles[...], NT, preferred_element_type=f32)
    low_out[...] = low_own[...].astype(bf16)
    loop(1, n_seq, lambda k: low_copy(k).start())
    loop(1, n_seq, lambda k: up_copy(k).start())
    up_all[0] = up[...]
    load_query.start()
    load_grad.start()
    for copy in (load_gain, load_gate, load_lengths, load_reader, load_doc):
        copy.wait()

    def find(g):
        at, mark = jnp.int32(0), jnp.int32(docs)
        for i in range(img_dev):
            hit = reader[i] == g
            at = jnp.where(hit, i, at)
            mark = jnp.where(hit, doc[i], mark)
        pick[g] = at
        tag[g] = mark

    loop(0, n_dp, find)

    part_rows = keys // PARTS
    slots = n_dp // PARTS

    def routed(n, into, b):
        skip = img_rows if b == 0 else 0
        part = into.at[pl.ds(b * part_rows + skip, part_rows - skip)]
        all_here(part, route_sem.at[n, b])

    def route(n, out, into, k):
        g = lax.rem(p + k, n_dp)
        return remote(
            out.at[k],
            into.at[pl.ds(pl.multiple_of(k * img_rows, img_rows), img_rows)],
            sent_sem.at[4 + n],
            route_sem.at[n, k // slots],
            (g, z),
        )

    def k_route(k):
        return route(0, k_out, k_all.at[0], k)

    def v_route(k):
        return route(1, v_out, v_all.at[0], k)

    def ext_route(k):
        return route(2, ext_out, ext, k)

    lane = lax.broadcasted_iota(jnp.int32, (img_rows, LANES), 1)

    def ext_block(g):
        mark = jnp.where(lane == rank + tag[g], 1.0, 0.0)
        low = ext_rows[pick[g]].astype(f32)
        return jnp.where(lane < rank, low, mark).astype(bf16)

    def send_ext(k):
        ext_out[k] = ext_block(lax.rem(p + k, n_dp))
        ext_route(k).start()

    def low_finish():
        all_sent(2, low_in.at[others])
        all_here(low_in.at[others], all_sem.at[1])
        low_total = low_own[...]
        for k in range(1, n_seq):
            low_total = low_total + low_in[k].astype(f32)
        low_rank = low_total.astype(bf16)
        low_out[...] = low_rank
        eye = lax.broadcasted_iota(jnp.int32, (rank, LANES), 0) == lax.broadcasted_iota(
            jnp.int32, (rank, LANES), 1
        )
        eye = jnp.where(eye, 1.0, 0.0).astype(bf16)
        low_rows = lax.dot_general(low_rank, eye, TN, preferred_element_type=f32)
        ext_rows[...] = low_rows.astype(bf16).reshape(img_dev, img_rows, LANES)

    for t in range(1, mid):
        if t == mid - 1:
            low_finish()
            loop(1, n_dp, send_ext)
            load_wv.wait()
            first_sums(1)
            first_sends(1)
        sum_step(0, t)
    if mid == 1:
        low_finish()
        loop(1, n_dp, send_ext)
        load_wv.wait()
        first_sums(1)
        first_sends(1)

    per_part = sum_rows // img_rows
    own[0] = own_part(0, z)
    for b in range(PARTS):
        key_raw = last_sums(0, b)
        mean_square = jnp.mean(key_raw * key_raw, axis=-1, keepdims=True)
        key_rows = (key_raw * lax.rsqrt(mean_square + EPS) * gain[...]).astype(bf16)
        rows_k[pl.ds(b * per_part, per_part)] = key_rows.reshape(per_part, img_rows, LANES)

    def send_k(k):
        k_out[k] = rows_k[pick[lax.rem(p + k, n_dp)]]
        k_route(k).start()

    loop(1, n_dp, send_k)
    k_all[0, :img_rows, :] = rows_k[pick[p]]
    ext[:img_rows, :] = ext_block(p)

    lane_tok = lax.broadcasted_iota(jnp.int32, (tokens, LANES), 1)
    place = lax.broadcasted_iota(jnp.int32, (tokens, LANES), 0) + z * tokens
    own_doc = jnp.zeros((tokens, LANES), jnp.int32)
    end = jnp.int32(0)
    for d in range(docs - 1):
        end = end + lengths[0, d]
        own_doc = own_doc + jnp.where(place >= end, 1, 0)
    other = (lane_tok >= rank) & (lane_tok <= rank + docs) & (lane_tok != rank + own_doc)
    penalty = jnp.where(other, MASKED, 0.0).astype(bf16)
    for n in range(block // tokens):
        bias[n * tokens : (n + 1) * tokens, :] = penalty
    small[...] = jnp.zeros_like(small)
    gate = jnp.tanh(jnp.full((1, LANES), gate_s[0], f32))
    all_here(up_all.at[others], all_sem.at[2])
    for b in range(PARTS):
        routed(2, ext, b)
    ext_t[...] = ext[...].T
    load_query.wait()
    load_grad.wait()

    for t in range(1, mid):
        sum_step(1, t)
    last = mid - 1

    def gather(held, n):
        def ahead(t, b):
            part = pl.ds(pl.multiple_of(b * part_rows, part_rows), part_rows)
            source, into = lax.rem(n_seq - t, n_seq), n_seq - 1 - t
            return remote(
                held.at[source, part],
                held.at[into, part],
                sent_sem.at[7 + n // 2],
                ring_sem.at[n, t, b],
                right,
            )

        def back(t, b):
            part = pl.ds(pl.multiple_of(b * part_rows, part_rows), part_rows)
            return remote(
                held.at[t, part],
                held.at[t + 1, part],
                sent_sem.at[7 + n // 2],
                ring_sem.at[n + 1, t, b],
                left,
            )

        return ((ahead, lambda b: b < PARTS // 2), (back, lambda b: b >= PARTS // 2))

    k_ways, v_ways = gather(k_all, 0), gather(v_all, 2)

    def gather_start(ways, n, held):
        for b in range(PARTS):
            routed(n, held.at[0], b)
            for way, whole in ways:
                if last > 0 or whole(b):
                    way(0, b).start()

    def forward(ways, t, b):
        for way, whole in ways:

            @pl.when((t <= last) | whole(b))
            def _():
                way(t - 1, b).wait_recv()

            @pl.when((t < last) | ((t == last) & whole(b)))
            def _():
                way(t, b).start()

    def after_block(ways, m, first_head):
        i = m // blocks
        step = (i + 1) // 2
        q = m - blocks * (2 * step - 1)
        per = PARTS // (2 * blocks)

        pl.when(m == blocks - 1)(first_head)

        @pl.when((i >= 1) & (i < n_seq - 1))
        def _():
            loop(q * per, (q + 1) * per, lambda b: forward(ways, step + 1, b))


    def send_v(k):
        v_out[k] = rows_v[pick[lax.rem(p + k, n_dp)]]
        v_route(k).start()

    def values_out():
        low_up = lax.dot_general(low_out[...], up[...], TN, preferred_element_type=f32)
        own[0] = own_part(1, z) + ADAPTER_SCALE * low_up
        for b in range(PARTS):
            value = last_sums(1, b).astype(bf16)
            rows_v[pl.ds(b * per_part, per_part)] = value.reshape(per_part, img_rows, LANES)
        v_all[0, :img_rows, :] = rows_v[pick[p]]
        for b in range(PARTS):
            forward(k_ways, 1, b)
            loop(max(1, b * slots), (b + 1) * slots, send_v)

    def values_on():
        loop(0, PARTS, lambda b: forward(v_ways, 1, b))

    def stack(ref, cols):
        part = ref[:, cols]
        return jnp.concatenate(
            [part[:, n * LANES : (n + 1) * LANES] for n in range(block // tokens)], axis=0
        )

    def unstack(x):
        return jnp.concatenate(
            [x[n * tokens : (n + 1) * tokens] for n in range(block // tokens)], axis=1
        )

    def where_is(m):
        i, j = m // blocks, lax.rem(m, blocks)
        slot = jnp.where(lax.rem(i, 2) == 1, n_seq - (i + 1) // 2, i // 2)
        head = lax.rem(z + slot, n_seq)
        cols = pl.ds(pl.multiple_of(head * head_width + j * span, span), span)
        return i, j, slot, head, cols

    def first_half(m):
        i, j, slot, head, cols = where_is(m)
        g = (gate * stack(grad, cols).astype(f32)).astype(bf16)
        grad[:, cols] = unstack(g)
        q = jnp.concatenate([stack(query, cols), bias[...]], axis=1)
        key_ext = jnp.concatenate([k_all[slot], ext[...]], axis=1)
        scores = lax.dot_general(q, key_ext, NT, preferred_element_type=f32)
        row_max = jnp.max(scores, axis=1, keepdims=True)
        weights = jnp.exp2((scores - row_max) * (scale * LOG2_E))
        prob = weights * (1.0 / jnp.sum(weights, axis=1, keepdims=True))
        prob = prob.astype(bf16)
        probs[i, pl.ds(pl.multiple_of(j * block, block), block), :] = prob
        part = lax.dot_general(g, prob, TN, preferred_element_type=f32)

        @pl.when(j == 0)
        def _():
            value_grad[...] = part

        @pl.when(j > 0)
        def _():
            value_grad[...] += part

        @pl.when(j == blocks - 1)
        def _():
            whole = value_grad[...].astype(bf16)
            small[:rank, :] += jnp.dot(
                up_all[lax.rem(n_seq - slot, n_seq)], whole, preferred_element_type=f32
            )
            small[rank:, lanes_of(head)] = lax.dot_general(
                ext_t[:rank, :], whole, NT, preferred_element_type=f32
            )

        after_block(k_ways, m, values_out)

        @pl.when(m == max(blocks * (2 * last - 1), blocks) - 1)
        def _():
            gather_start(v_ways, 1, v_all)

    gather_start(k_ways, 0, k_all)
    loop(0, n_seq * blocks, first_half)

    def col_copy(k):
        target = lax.rem(z + k, n_seq)
        return remote(
            small.at[:, lanes_of(target)], col_in.at[k], sent_sem.at[9], all_sem.at[3], (p, target)
        )

    wide = total.shape[1]

    def back_copy(n):
        j, s = lax.rem(n, fit), n // fit
        o = lax.rem(p + n_dp - fit * z - j, n_dp)
        into = back_in.at[fit * z + j]
        return remote(back_out.at[j], into, sent_sem.at[10], all_sem.at[4], (o, s))

    def stage_copy(r, k, send):
        stride, size = stages[r]
        digit = lax.rem(p // stride, size)
        peer = lax.rem(digit + k, size)
        slot = digit if send else lax.rem(digit + size - k, size)
        return remote(
            stage_out[r],
            stage_in[r].at[slot],
            sent_sem.at[12 + r],
            stage_sem.at[r, k],
            (p + (peer - digit) * stride, z),
        )

    def stage_start(r):
        stride, size = stages[r]
        stage_out[r][...] = total[...].astype(bf16)
        stage_in[r][lax.rem(p // stride, size)] = stage_out[r][...]
        for k in range(1, size):
            stage_copy(r, k, True).start()

    def stage_finish(r):
        size = stages[r][1]
        for k in range(1, size):
            stage_copy(r, k, False).wait_recv()
        here = stage_in[r][0].astype(f32)
        for d in range(1, size):
            here = here + stage_in[r][d].astype(f32)
        total[...] = here
        if r + 1 < len(stages):
            stage_start(r + 1)

    def adapter_back():
        mine = small[:, lanes_of(z)]
        all_here(col_in.at[others], all_sem.at[3])
        for k in range(1, n_seq):
            mine = mine + col_in[k]
        mine = ADAPTER_SCALE * mine
        for j in range(fit):
            moved = mine[:rank]
            if j > 0:
                moved = pltpu.roll(moved, LANES - j * img_rows, 1)
            back_out[j] = moved.astype(bf16)
        total[:, width:] = jnp.zeros((rank, wide - width), f32)
        total[:, wide - LANES :] = mine[rank:]
        loop(1, fit * n_seq, lambda n: back_copy(n).start())

        @pl.when(z == 0)
        def _():
            back_in[0] = back_out[0]

        @pl.when(z != 0)
        def _():
            back_copy(0).start()

    def adapter_sum():
        @pl.when(z == 0)
        def _():
            all_here(back_in.at[pl.ds(1, n_dp - 1)], all_sem.at[4])

        @pl.when(z != 0)
        def _():
            all_here(back_in, all_sem.at[4])

        lane_rank = lax.broadcasted_iota(jnp.int32, (rank, LANES), 1)
        pieces_in = []
        for first in range(0, img_dev, fit):
            piece = jnp.zeros((rank, LANES), f32)
            for i in range(fit):
                slot = lax.rem(reader[first + i] - p + n_dp, n_dp)
                held = back_in[slot].astype(f32)
                if i > 0:
                    held = pltpu.roll(held, i * img_rows, 1)
                piece = jnp.where(lane_rank // img_rows == i, held, piece)
            pieces_in.append(piece.astype(bf16))
        total[:, :width] = jnp.dot(
            jnp.concatenate(pieces_in, axis=1), tiles[...], preferred_element_type=f32
        )
        stage_start(0)

    loop(1, n_seq, lambda k: col_copy(k).start())

    def store(n, head):
        cols = lanes_of(head, head_width)
        source, into = ((gated, gated_hbm), (query_grad, query_grad_hbm))[n]
        return pltpu.make_async_copy(source.at[:, cols], into.at[:, cols], store_sem.at[n])

    end_block = n_seq * blocks - 1

    def second_half(m):
        i, j, slot, head, cols = where_is(m)
        g = stack(grad, cols)
        prob = probs[i, pl.ds(pl.multiple_of(j * block, block), block), :]
        value = v_all[slot]
        attended = jnp.dot(prob, value, preferred_element_type=f32)
        prob_grad = lax.dot_general(g, value, NT, preferred_element_type=f32)
        gated[:, cols] = unstack((gate * attended).astype(bf16))
        delta = jnp.sum(g.astype(f32) * attended, axis=1, keepdims=True)
        score_grad = (prob.astype(f32) * (prob_grad - delta)).astype(bf16)
        out_grad = jnp.dot(score_grad, k_all[slot], preferred_element_type=f32)
        query_grad[:, cols] = unstack((out_grad * scale).astype(bf16))

        @pl.when(j == blocks - 1)
        def _():
            store(0, head).start()
            store(1, head).start()

        after_block(v_ways, m, values_on)
        events = [adapter_back, adapter_sum]
        events += [functools.partial(stage_finish, r) for r in range(len(stages) - 1)]
        for at, event in zip(EVENTS, events):
            pl.when(m == min(at, end_block))(event)

    loop(0, n_seq * blocks, second_half)

    stage_finish(len(stages) - 1)
    down_stage[...] = total[:, :width]
    up_stage[...] = total[:, wide - LANES :]
    store_down = pltpu.make_async_copy(down_stage, down_hbm, store_sem.at[2])
    store_up = pltpu.make_async_copy(up_stage, up_out_hbm, store_sem.at[3])
    store_down.start()
    store_up.start()

    most = pl.ds(0, n_seq - 1)
    all_sent(0, sum_k.at[most])
    all_sent(1, sum_v.at[most])
    all_sent(3, up_all.at[others])
    for n, out in enumerate((k_out, v_out, ext_out)):
        all_sent(4 + n, out.at[pl.ds(1, n_dp - 1)])
    all_sent(7, k_all.at[most])
    all_sent(8, v_all.at[most])
    all_sent(9, col_in.at[others])

    @pl.when(z == 0)
    def _():
        all_sent(10, back_in.at[pl.ds(1, n_dp - 1)])

    @pl.when(z != 0)
    def _():
        all_sent(10, back_in)

    for r, (stride, size) in enumerate(stages):
        all_sent(12 + r, stage_in[r].at[pl.ds(0, size - 1)])
    pltpu.make_async_copy(gated, gated_hbm, store_sem.at[0]).wait()
    pltpu.make_async_copy(query_grad, query_grad_hbm, store_sem.at[1]).wait()
    store_down.wait()
    store_up.wait()


def per_device(
    queries,
    output_gradient,
    tiles,
    frozen_key_weight,
    frozen_value_weight,
    key_norm_gain,
    adapter_down_weight,
    adapter_up_weight,
    gate,
    document_lengths,
    image_reader_group,
    image_document,
):
    n_dp, n_seq = lax.axis_size("dp"), lax.axis_size("seq")
    docs = document_lengths.shape[1]
    rank = adapter_up_weight.shape[0]
    img_dev, img_rows, width = tiles.shape
    rows = img_dev * img_rows
    tokens, columns = queries.shape
    keys = n_dp * img_rows
    block = min(HEADS_AT_ONCE * LANES, columns // n_seq) // LANES * tokens
    wide = -(-width // LANES) * LANES + LANES
    stages = stages_of(n_dp)
    fit = LANES // img_rows
    any_space = pl.BlockSpec(memory_space=pl.ANY)
    f32, bf16 = jnp.float32, jnp.bfloat16

    def held(*shape, kind=bf16):
        return pltpu.VMEM(shape, kind)

    dma = pltpu.SemaphoreType.DMA
    gated, query_grad, down_rows, up_grad = pl.pallas_call(
        functools.partial(fused_kernel, n_dp, n_seq, docs, stages),
        out_shape=(
            jax.ShapeDtypeStruct((tokens, columns), bf16),
            jax.ShapeDtypeStruct((tokens, columns), bf16),
            jax.ShapeDtypeStruct((rank, width), f32),
            jax.ShapeDtypeStruct((rank, LANES), f32),
        ),
        in_specs=[any_space] * 12,
        out_specs=(any_space,) * 4,
        scratch_shapes=[
            held(tokens, columns),
            held(tokens, columns),
            held(tokens, columns),
            held(tokens, columns),
            held(rows, width),
            held(width, n_seq * LANES),
            held(width, n_seq * LANES),
            held(rank, width),
            held(rank, LANES),
            held(1, LANES, kind=f32),
            pltpu.SMEM((1,), f32),
            pltpu.SMEM((1, docs), jnp.int32),
            pltpu.SMEM((img_dev,), jnp.int32),
            pltpu.SMEM((img_dev,), jnp.int32),
            held(2, rows, LANES, kind=f32),
            held(n_seq + 2, rows, LANES, kind=f32),
            held(n_seq + 2, rows, LANES),
            held(rank, rows, kind=f32),
            held(rank, rows),
            held(n_seq, rank, rows),
            held(n_seq, rank, LANES),
            pltpu.SMEM((n_dp,), jnp.int32),
            pltpu.SMEM((n_dp,), jnp.int32),
            held(img_dev, img_rows, LANES),
            held(img_dev, img_rows, LANES),
            held(img_dev, img_rows, LANES),
            held(n_dp, img_rows, LANES),
            held(n_dp, img_rows, LANES),
            held(n_dp, img_rows, LANES),
            held(n_seq, keys, LANES),
            held(n_seq, keys, LANES),
            held(keys, LANES),
            held(LANES, keys),
            held(block, LANES),
            held(n_seq, columns // n_seq // LANES * tokens, keys),
            held(LANES, keys, kind=f32),
            held(2 * rank, keys, kind=f32),
            held(n_seq, 2 * rank, LANES, kind=f32),
            held(fit, rank, LANES),
            held(n_dp, rank, LANES),
            held(rank, wide, kind=f32),
            [held(rank, wide) for stage in stages],
            [held(size, rank, wide) for stride, size in stages],
            held(rank, width, kind=f32),
            held(rank, LANES, kind=f32),
            dma((12,)),
            dma((4,)),
            dma((15,)),
            dma((6,)),
            dma((2, 2, n_seq // 2, PARTS)),
            dma((3, PARTS)),
            dma((4, n_seq // 2, PARTS)),
            dma((len(stages), 8)),
        ],
        compiler_params=pltpu.CompilerParams(
            collective_id=0, has_side_effects=True, vmem_limit_bytes=58 << 20
        ),
    )(
        queries,
        output_gradient,
        tiles.reshape(rows, width),
        frozen_key_weight,
        frozen_value_weight,
        adapter_down_weight.T,
        adapter_up_weight,
        key_norm_gain.reshape(1, -1),
        gate,
        document_lengths,
        image_reader_group,
        image_document,
    )
    return (gated, query_grad, down_rows.T, up_grad)


def solution(mesh):
    placed = (
        P(("dp", "seq"), None),
        P(("dp", "seq"), None),
        P("dp", None, "seq"),
        P("seq", None),
        P("seq", None),
        P(),
        P("seq", None),
        P(None, "seq"),
        P(),
        P("dp", None),
        P("dp"),
        P("dp"),
    )
    return jax.shard_map(
        per_device,
        mesh=mesh,
        in_specs=placed,
        out_specs=(P(("dp", "seq"), None), P(("dp", "seq"), None), P("seq", None), P(None, "seq")),
        check_vma=False,
    )
```
